32 devices in a mesh: dp: 16 (over z, y, core), freq: 2 (over x).
Axes of the slice: x: 2, y: 2, z: 4, core: 2. Of those that a mesh axis runs over, the one named last changes fastest.
Arguments:
- pixels: bfloat16 [256, 256, 3328], P('dp', None, 'freq'), may hold values from -6 to 6
- band_group: int32 [256], P('dp'), may hold values from 0 to 1
- mask_order: int32 [256, 256], P('dp'), may hold values from 0 to 255, each once within a row
- visible_count: int32 [256], P('dp'), may hold values from 32 to 64, as said below
- scale_id: int32 [256], P('dp'), may hold values from 0 to 3
- patch_weight: bfloat16 [2, 3328, 1024], P(None, 'freq'), may hold values from -0.109375 to 0.109375
- enc_qkv: bfloat16 [1024, 3, 1024], P(None, None, 'freq'), may hold values from -0.1875 to 0.1875
- enc_out: bfloat16 [1024, 1024], P('freq'), may hold values from -0.375 to 0.375
- enc_up: bfloat16 [1024, 4096], P(None, 'freq'), may hold values from -0.1875 to 0.1875
- enc_down: bfloat16 [4096, 1024], P('freq'), may hold values from -0.09375 to 0.09375
- enc_gains: float32 [3, 1024], replicated, may hold values from 0.25 to 1.75
- enc_biases: float32 [3, 1024], replicated, may hold values from -3 to 3
- dec_embed: bfloat16 [1024, 512], replicated, may hold values from -0.1875 to 0.1875
- mask_token: float32 [512], replicated, may hold values from -5 to 5
- dec_qkv: bfloat16 [512, 3, 512], P(None, None, 'freq'), may hold values from -0.25 to 0.25
- dec_out: bfloat16 [512, 512], P('freq'), may hold values from -0.5 to 0.5
- dec_up: bfloat16 [512, 2048], P(None, 'freq'), may hold values from -0.25 to 0.25
- dec_down: bfloat16 [2048, 512], P('freq'), may hold values from -0.125 to 0.125
- dec_gains: float32 [3, 512], replicated, may hold values from 0.25 to 1.75
- dec_biases: float32 [3, 512], replicated, may hold values from -3 to 3
- head_weight: bfloat16 [512, 6656], P(None, 'freq'), may hold values from -0.25 to 0.25
- recon_cotangent: bfloat16 [256, 256, 6656], P('dp', None, 'freq'), may hold values from -6 to 6
Outputs:
- reconstructions: bfloat16 [256, 256, 6656], P('dp', None, 'freq')
- pixel_grad: float32 [256, 256, 3328], P('dp', None, 'freq')
- patch_weight_grad: float32 [2, 3328, 1024], P(None, 'freq')
- enc_qkv_grad: float32 [1024, 3, 1024], P(None, None, 'freq')
- enc_out_grad: float32 [1024, 1024], P('freq')
- enc_up_grad: float32 [1024, 4096], P(None, 'freq')
- enc_down_grad: float32 [4096, 1024], P('freq')
- enc_gains_grad: float32 [3, 1024], replicated
- enc_biases_grad: float32 [3, 1024], replicated
- dec_embed_grad: float32 [1024, 512], replicated
- mask_token_grad: float32 [512], replicated
- dec_qkv_grad: float32 [512, 3, 512], P(None, None, 'freq')
- dec_out_grad: float32 [512, 512], P('freq')
- dec_up_grad: float32 [512, 2048], P(None, 'freq')
- dec_down_grad: float32 [2048, 512], P('freq')
- dec_gains_grad: float32 [3, 512], replicated
- dec_biases_grad: float32 [3, 512], replicated
- head_weight_grad: float32 [512, 6656], P(None, 'freq')
The draws below stay inside these ranges and needn't reach their ends.
Inputs may be any that keep to these rules, and one draw needn't show every extreme that they name: `visible_count`: every image has at least 32 and at most 64 visible patches, and in each aligned block of 16 images at least one image has 64.
All inputs are finite; a program needn't handle non-finite values.
Results may differ from the reference program's by a relative error of at most 0.035.
Values may be sent and summed in bfloat16 or wider, within the bound.
A program may use at most 512 MiB of HBM per device.

```python
import math
import jax
import jax.numpy as jnp
from jax import lax

D = 1024
HEADS = 16
FF = 4096
DDEC = 512
DHEADS = 16
DFF = 2048
PIX = 3328
RGB_PIX = 768
GROUPS = 2
SCALES = 4
SIDE = 16
NPATCH = 256
VIS = 64
IMAGES_DEV = 16
IMAGES = 256


def draw_visible_count(key, part):
    key = jax.random.fold_in(key, 7)
    first, second = jax.random.split(key)
    counts = jax.random.randint(first, (IMAGES,), VIS // 2, VIS + 1)
    blocks = IMAGES // IMAGES_DEV
    chosen = jax.random.randint(second, (blocks,), 0, IMAGES_DEV) + jnp.arange(blocks) * IMAGES_DEV
    return counts.at[chosen].set(VIS).astype(jnp.int32)


def with_ends(result, own_key, low, largest):
    place = [jax.random.randint(jax.random.fold_in(own_key, axis), (), 0, length) for axis, length in enumerate(result.shape)]
    widest = result.shape.index(max(result.shape))
    neighbour = place[:widest] + [(place[widest] + 1) % result.shape[widest]] + place[widest + 1:]
    return result.at[tuple(place)].set(low).at[tuple(neighbour)].set(largest)


def levels(rng, extent, cuts, low, high):
    def one(position, blocks):
        draws = jax.random.uniform(jax.random.fold_in(jax.random.fold_in(rng, 6), position), (blocks,), jnp.float32, low / len(cuts), high / len(cuts))
        return jnp.repeat(jnp.exp(draws), extent[position] // blocks).reshape((-1,) + (1,) * (len(extent) - position - 1))

    factor_of = one(*cuts[0])
    for cut in cuts[1:]:
        factor_of = factor_of * one(*cut)
    return factor_of


def bell_draw(stream_key, shape, width, bound, shards=(), kind=jnp.bfloat16):
    loudness = levels(stream_key, shape, shards, -0.22, 0.18) if shards else 1.0
    drawn = jax.random.normal(stream_key, shape, jnp.float32) * width * loudness
    return jnp.minimum(jnp.maximum(drawn, -bound), bound).astype(kind)


def setup_inputs(seed: int = 0) -> dict:
    arg_keys = jax.random.split(jax.random.key(seed), 23)
    return {
        "pixels": bell_draw(arg_keys[0], (IMAGES, NPATCH, PIX), 1.0, 6.0, ((0, 16), (2, 2))),
        "band_group": with_ends(jax.random.randint(arg_keys[1], (IMAGES,), 0, GROUPS), jax.random.fold_in(arg_keys[1], 1), 0, GROUPS - 1).astype(jnp.int32),
        "mask_order": jax.vmap(lambda own: jax.random.permutation(own, NPATCH))(jax.random.split(arg_keys[2], IMAGES)).reshape((IMAGES, NPATCH)).astype(jnp.int32),
        "visible_count": draw_visible_count(jax.random.fold_in(arg_keys[22], 71), 0),
        "scale_id": with_ends(jax.random.randint(arg_keys[4], (IMAGES,), 0, SCALES), jax.random.fold_in(arg_keys[4], 1), 0, SCALES - 1).astype(jnp.int32),
        "patch_weight": bell_draw(arg_keys[5], (GROUPS, PIX, D), PIX ** -0.5, 0.109375, ((1, 2),)),
        "enc_qkv": bell_draw(arg_keys[6], (D, 3, D), D ** -0.5, 0.1875, ((2, 2),)),
        "enc_out": bell_draw(arg_keys[7], (D, D), (D // 4) ** -0.5, 0.375, ((0, 2),)),
        "enc_up": bell_draw(arg_keys[8], (D, FF), D ** -0.5, 0.1875, ((1, 2),)),
        "enc_down": bell_draw(arg_keys[9], (FF, D), FF ** -0.5, 0.09375, ((0, 2),)),
        "enc_gains": jnp.clip(1.0 + 0.15 * jax.random.normal(arg_keys[10], (3, D), jnp.float32), 0.25, 1.75),
        "enc_biases": bell_draw(arg_keys[11], (3, D), 0.3, 3.0, (), jnp.float32),
        "dec_embed": bell_draw(arg_keys[12], (D, DDEC), D ** -0.5, 0.1875),
        "mask_token": bell_draw(arg_keys[13], (DDEC,), 1.0, 5.0, (), jnp.float32),
        "dec_qkv": bell_draw(arg_keys[14], (DDEC, 3, DDEC), DDEC ** -0.5, 0.25, ((2, 2),)),
        "dec_out": bell_draw(arg_keys[15], (DDEC, DDEC), (DDEC // 4) ** -0.5, 0.5, ((0, 2),)),
        "dec_up": bell_draw(arg_keys[16], (DDEC, DFF), DDEC ** -0.5, 0.25, ((1, 2),)),
        "dec_down": bell_draw(arg_keys[17], (DFF, DDEC), DFF ** -0.5, 0.125, ((0, 2),)),
        "dec_gains": jnp.clip(1.0 + 0.15 * jax.random.normal(arg_keys[18], (3, DDEC), jnp.float32), 0.25, 1.75),
        "dec_biases": bell_draw(arg_keys[19], (3, DDEC), 0.3, 3.0, (), jnp.float32),
        "head_weight": bell_draw(arg_keys[20], (DDEC, 2 * PIX), DDEC ** -0.5, 0.25, ((1, 2),)),
        "recon_cotangent": bell_draw(arg_keys[21], (IMAGES, NPATCH, 2 * PIX), 1.0, 6.0, ((0, 16), (2, 2))),
    }


@jax.custom_vjp
def low(v):
    return lax.optimization_barrier(v.astype(jnp.bfloat16)).astype(jnp.float32)

@jax.custom_vjp
def low_back(v):
    return v

def low_keep(v):
    return (low(v), None)

def low_pass(kept, grad):
    return (grad,)

def back_keep(v):
    return (v, None)

def back_low(kept, grad):
    return (low(grad),)
low.defvjp(low_keep, low_pass)
low_back.defvjp(back_keep, back_low)
HIGHEST = lax.Precision.HIGHEST
EPSILON = 1e-06
MASKED = -1e+30

def layer_norm(values, scales, shifts):
    center = values - lax.optimization_barrier(jnp.mean(values, -1, keepdims=True))
    spread = lax.optimization_barrier(jnp.mean(center * center, -1, keepdims=True))
    return center * lax.rsqrt(spread + EPSILON) * scales + shifts

def position_code(patch_ids, ratios, features):
    quarter = features // 4
    index_f = jnp.arange(quarter, dtype=jnp.float32)
    frequencies = jnp.exp(index_f * (-math.log(10000.0) / quarter))
    row_angle = ((patch_ids // SIDE).astype(jnp.float32) * ratios)[..., None] * frequencies
    col_angle = ((patch_ids % SIDE).astype(jnp.float32) * ratios)[..., None] * frequencies
    return jnp.concatenate([jnp.sin(row_angle), jnp.cos(row_angle), jnp.sin(col_angle), jnp.cos(col_angle)], -1)

def attention(normed, weight_qkv, weight_out, head_count, valid_keys):
    images, seq_len, features = normed.shape
    head_size = features // head_count
    project = jnp.einsum('blw,wcn->blcn', normed, weight_qkv, precision=HIGHEST)
    queries = low(low_back(project[:, :, 0]) * head_size ** (-0.5))
    keys_all = low(low_back(project[:, :, 1]))
    values_all = low(low_back(project[:, :, 2]))
    shape4 = (images, seq_len, head_count, head_size)
    scores = jnp.einsum('bshd,bthd->bhst', queries.reshape(shape4), keys_all.reshape(shape4), precision=HIGHEST)
    scores = jnp.where(valid_keys[:, None, None, :], low_back(scores), MASKED)
    weights = low(jax.nn.softmax(scores, axis=-1))
    mixed_rows = jnp.einsum('bhst,bthd->bshd', weights, values_all.reshape(shape4), precision=HIGHEST)
    mixed_rows = low(low_back(mixed_rows.reshape(images, seq_len, features)))
    return low_back(jnp.einsum('blw,wv->blv', mixed_rows, weight_out, precision=HIGHEST))

def feed_forward(normed, weight_up, weight_down):
    pre_act = low_back(jnp.einsum('blw,wf->blf', normed, weight_up, precision=HIGHEST))
    active = low(jax.nn.gelu(pre_act, approximate=False))
    return low_back(jnp.einsum('blf,fw->blw', active, weight_down, precision=HIGHEST))

def forward_group(params, pixels, band_group, mask_order, visible_count, scale_id):
    patch_weight, enc_qkv, enc_out, enc_up, enc_down, enc_gains, enc_biases, dec_embed, mask_token, dec_qkv, dec_out, dec_up, dec_down, dec_gains, dec_biases, head_weight = params
    columns = jnp.arange(PIX)
    multi_band = band_group == 0
    keep_band = (multi_band[:, None] | (columns[None, :] < RGB_PIX)).astype(jnp.float32)
    slot_ids = mask_order[:, :VIS]
    select = (slot_ids[:, :, None] == jnp.arange(NPATCH)[None, None, :]).astype(jnp.float32)
    picked = jnp.einsum('bsp,bpc->bsc', select, pixels * keep_band[:, None, :], precision=HIGHEST)
    multi_f = multi_band.astype(jnp.float32)[:, None, None]
    embedded = jnp.einsum('bsc,cd->bsd', picked * multi_f, patch_weight[0], precision=HIGHEST)
    embedded = embedded + jnp.einsum('bsc,cd->bsd', picked * (1.0 - multi_f), patch_weight[1], precision=HIGHEST)
    ratios = jnp.exp2(scale_id.astype(jnp.float32) - 1.0)[:, None]
    stream = low_back(embedded) + position_code(slot_ids, ratios, D)
    valid_enc = jnp.arange(VIS)[None, :] < visible_count[:, None]
    stream = stream + attention(low(layer_norm(stream, enc_gains[0], enc_biases[0])), enc_qkv, enc_out, HEADS, valid_enc)
    stream = stream + feed_forward(low(layer_norm(stream, enc_gains[1], enc_biases[1])), enc_up, enc_down)
    latent = low(layer_norm(stream, enc_gains[2], enc_biases[2]))
    lifted = low_back(jnp.einsum('bsd,de->bse', latent, dec_embed, precision=HIGHEST))
    live_select = select * valid_enc.astype(jnp.float32)[:, :, None]
    shown_mask = lax.optimization_barrier(jnp.sum(live_select, axis=1))[:, :, None]
    decoded = jnp.einsum('bsp,bse->bpe', live_select, lifted, precision=HIGHEST) + (1.0 - shown_mask) * mask_token
    decoded = decoded + position_code(jnp.arange(NPATCH)[None, :], ratios, DDEC)
    valid_dec = jnp.ones((pixels.shape[0], NPATCH), dtype=bool)
    decoded = decoded + attention(low(layer_norm(decoded, dec_gains[0], dec_biases[0])), dec_qkv, dec_out, DHEADS, valid_dec)
    decoded = decoded + feed_forward(low(layer_norm(decoded, dec_gains[1], dec_biases[1])), dec_up, dec_down)
    final_rows = low(layer_norm(decoded, dec_gains[2], dec_biases[2]))
    return jnp.einsum('bpe,ec->bpc', final_rows, head_weight, precision=HIGHEST)

def reference(pixels, band_group, mask_order, visible_count, scale_id, patch_weight, enc_qkv, enc_out, enc_up, enc_down, enc_gains, enc_biases, dec_embed, mask_token, dec_qkv, dec_out, dec_up, dec_down, dec_gains, dec_biases, head_weight, recon_cotangent):
    params = tuple((weight_arg.astype(jnp.float32) for weight_arg in (patch_weight, enc_qkv, enc_out, enc_up, enc_down, enc_gains, enc_biases, dec_embed, mask_token, dec_qkv, dec_out, dec_up, dec_down, dec_gains, dec_biases, head_weight)))
    blocks = IMAGES // IMAGES_DEV

    def split_blocks(values):
        return values.reshape((blocks, IMAGES_DEV) + values.shape[1:])
    integer_args = (split_blocks(band_group), split_blocks(mask_order), split_blocks(visible_count), split_blocks(scale_id))
    step_fn = jax.checkpoint(lambda weights, arrays: forward_group(weights, *arrays))

    def whole_run(weights, pixels32):
        return lax.map(lambda arrays: step_fn(weights, arrays), (pixels32,) + integer_args)
    recon_all, pull_back = jax.vjp(whole_run, params, split_blocks(pixels.astype(jnp.float32)))
    weight_grads, pixel_grad = pull_back(split_blocks(recon_cotangent.astype(jnp.float32)))
    return (recon_all.reshape(IMAGES, NPATCH, 2 * PIX).astype(jnp.bfloat16), pixel_grad.reshape(IMAGES, NPATCH, PIX)) + tuple(weight_grads)
```

```python
import math

import jax
import jax.numpy as jnp
from jax import lax
from jax.experimental import pallas as pl
from jax.experimental.pallas import tpu as pltpu
from jax.sharding import PartitionSpec as P

D = 1024
HDIM = 64
DDEC = 512
DHDIM = 32
RGB_PIX = 768
SIDE = 16
NPATCH = 256
VIS = 64

HIGHEST = lax.Precision.HIGHEST
EPSILON = 1e-06
MASKED = -1e30
BF16 = jnp.bfloat16
F32 = jnp.float32
LANES = 128
VMEM_LIMIT = 48 * 1024 * 1024
MESH = pl.DeviceIdType.MESH


def dot(left, right):
    return jnp.dot(left, right, preferred_element_type=F32)


def dot_tn(left, right):
    return lax.dot_general(left, right, (((0,), (0,)), ((), ())), preferred_element_type=F32)


def dot_nt(left, right):
    return lax.dot_general(left, right, (((1,), (1,)), ((), ())), preferred_element_type=F32)


def normalize(values):
    center = values - jnp.mean(values, -1, keepdims=True)
    rstd = lax.rsqrt(jnp.mean(center * center, -1, keepdims=True) + EPSILON)
    return center * rstd, rstd


def layer_norm(values, scales, shifts):
    return (normalize(values)[0] * scales + shifts).astype(BF16)


def layer_norm_back(grad, values, scales):
    unit, rstd = normalize(values)
    scaled = grad * scales
    mean_grad = jnp.mean(scaled, -1, keepdims=True)
    mean_along = jnp.mean(scaled * unit, -1, keepdims=True)
    grad_in = rstd * (scaled - mean_grad - unit * mean_along)
    return grad_in, jnp.sum(grad * unit, 0), jnp.sum(grad, 0)


def code_tables(ratios, features):
    quarter = features // 4
    index_f = jnp.arange(quarter, dtype=F32)
    frequencies = jnp.exp(index_f * (-math.log(10000.0) / quarter))
    places = jnp.arange(SIDE).astype(F32)
    angle = (places[None, :] * ratios[:, None])[..., None] * frequencies
    return jnp.concatenate([jnp.sin(angle), jnp.cos(angle)], -1)


def slot_codes(slot_ids, ratios, features):
    table = code_tables(ratios, features)
    places = jnp.arange(SIDE)
    row = (slot_ids[..., None] // SIDE == places).astype(F32)
    col = (slot_ids[..., None] % SIDE == places).astype(F32)
    pick = lambda one_hot: jnp.einsum("bsp,bpf->bsf", one_hot, table, precision=HIGHEST)
    return jnp.concatenate([pick(row), pick(col)], -1)


def grid_codes(ratios, features):
    table = code_tables(ratios, features)
    images, _, half = table.shape
    row = jnp.broadcast_to(table[:, :, None, :], (images, SIDE, SIDE, half))
    col = jnp.broadcast_to(table[:, None, :, :], (images, SIDE, SIDE, half))
    return jnp.concatenate([row, col], -1).reshape(images, NPATCH, features)


def head_masks(group, head_size):
    lane = lax.broadcasted_iota(jnp.int32, (1, group), 1)
    return [(lane // head_size == h) for h in range(group // head_size)]


def masked_scores(keys, queries, valid):
    scores = dot_nt(keys, queries)
    if valid is not None:
        scores = jnp.where(valid, scores, MASKED)
    return scores


def attend_kernel(head_size, masked, count_ref, q_ref, k_ref, v_ref, o_ref):
    seq, width = q_ref.shape
    group = LANES
    valid = None
    if masked:
        valid = lax.broadcasted_iota(jnp.int32, (seq, seq), 0) < count_ref[pl.program_id(0)]
    masks = head_masks(group, head_size)
    for g in range(width // group):
        lanes = slice(g * group, (g + 1) * group)
        queries, keys, values = q_ref[:, lanes], k_ref[:, lanes], v_ref[:, lanes]
        values_t = jnp.transpose(values)
        parts = []
        for h, mask in enumerate(masks):
            scores = masked_scores(keys, jnp.where(mask, queries, 0).astype(BF16), valid)
            top = jnp.max(scores, 0, keepdims=True)
            power = jnp.exp(scores - top)
            total = jnp.sum(power, 0, keepdims=True)
            rows = slice(h * head_size, (h + 1) * head_size)
            parts.append(dot(values_t[rows], power.astype(BF16)) * (1.0 / total))
        mixed = jnp.concatenate(parts, 0)
        o_ref[:, lanes] = jnp.transpose(mixed).astype(BF16)


def attend_back_kernel(
    head_size, masked, count_ref, q_ref, k_ref, v_ref, g_ref, dq_ref, dk_ref, dv_ref
):
    seq, width = q_ref.shape
    group = LANES
    factor = head_size ** (-0.5)
    valid = None
    if masked:
        valid = lax.broadcasted_iota(jnp.int32, (seq, seq), 0) < count_ref[pl.program_id(0)]
    masks = head_masks(group, head_size)
    for g in range(width // group):
        lanes = slice(g * group, (g + 1) * group)
        queries, keys, values, grads = (
            q_ref[:, lanes],
            k_ref[:, lanes],
            v_ref[:, lanes],
            g_ref[:, lanes],
        )
        keys_t = jnp.transpose(keys)
        dq_parts = []
        dk_sum = jnp.zeros((seq, group), F32)
        dv_sum = jnp.zeros((seq, group), F32)
        for h, mask in enumerate(masks):
            own_q = jnp.where(mask, queries, 0).astype(BF16)
            own_g = jnp.where(mask, grads, 0).astype(BF16)
            scores = masked_scores(keys, own_q, valid)
            top = jnp.max(scores, 0, keepdims=True)
            power = jnp.exp(scores - top)
            weights = power * (1.0 / jnp.sum(power, 0, keepdims=True))
            dv_sum += dot(weights.astype(BF16), own_g)
            grad_weights = dot_nt(values, own_g)
            along = jnp.sum(weights * grad_weights, 0, keepdims=True)
            grad_scores = (weights * (grad_weights - along)).astype(BF16)
            dk_sum += dot(grad_scores, own_q)
            rows = slice(h * head_size, (h + 1) * head_size)
            dq_parts.append(dot(keys_t[rows], grad_scores) * factor)
        dq_ref[:, lanes] = jnp.transpose(jnp.concatenate(dq_parts, 0)).astype(BF16)
        dk_ref[:, lanes] = dk_sum.astype(BF16)
        dv_ref[:, lanes] = dv_sum.astype(BF16)


def attention_call(kernel, counts, arrays, seq, n_out, head_size, flop_factor):
    rows, width = arrays[0].shape
    images = rows // seq
    block = pl.BlockSpec((seq, width), lambda i, counts: (i, 0))
    out = jax.ShapeDtypeStruct((rows, width), BF16)
    return pl.pallas_call(
        kernel,
        grid_spec=pltpu.PrefetchScalarGridSpec(
            num_scalar_prefetch=1,
            grid=(images,),
            in_specs=[block] * len(arrays),
            out_specs=[block] * n_out,
        ),
        out_shape=[out] * n_out,
        compiler_params=pltpu.CompilerParams(vmem_limit_bytes=VMEM_LIMIT),
        cost_estimate=pl.CostEstimate(
            flops=flop_factor * rows * seq * width * (LANES // head_size),
            bytes_accessed=(len(arrays) + n_out) * rows * width * 2,
            transcendentals=rows * seq * width // head_size,
        ),
    )(counts, *arrays)


def attend(queries, keys, values, counts, seq, head_size, masked):
    kernel = lambda *refs: attend_kernel(head_size, masked, *refs)
    return attention_call(kernel, counts, [queries, keys, values], seq, 1, head_size, 4)[0]


def attend_back(queries, keys, values, grads, counts, seq, head_size, masked):
    kernel = lambda *refs: attend_back_kernel(head_size, masked, *refs)
    return attention_call(kernel, counts, [queries, keys, values, grads], seq, 3, head_size, 10)


def up_kernel(x_ref, w_ref, active_ref, slope_ref):
    pre = dot(x_ref[...], w_ref[...])
    cdf = 0.5 + 0.5 * lax.erf(pre * math.sqrt(0.5))
    density = jnp.exp(-0.5 * pre * pre) * (1.0 / math.sqrt(2.0 * math.pi))
    active_ref[...] = (pre * cdf).astype(BF16)
    slope_ref[...] = (cdf + pre * density).astype(BF16)


def up_projection(rows_in, weight):
    rows, depth = rows_in.shape
    width = weight.shape[1]
    row_block = math.gcd(rows, 512)
    col_block = math.gcd(width, 512)
    out = jax.ShapeDtypeStruct((rows, width), BF16)
    spec = pl.BlockSpec((row_block, col_block), lambda i, j: (i, j))
    return pl.pallas_call(
        up_kernel,
        grid=(rows // row_block, width // col_block),
        in_specs=[
            pl.BlockSpec((row_block, depth), lambda i, j: (i, 0)),
            pl.BlockSpec((depth, col_block), lambda i, j: (0, j)),
        ],
        out_specs=[spec, spec],
        out_shape=[out, out],
        compiler_params=pltpu.CompilerParams(vmem_limit_bytes=VMEM_LIMIT),
        cost_estimate=pl.CostEstimate(
            flops=2 * rows * depth * width,
            bytes_accessed=2 * (rows * depth + depth * width + 2 * rows * width),
            transcendentals=2 * rows * width,
        ),
    )(rows_in, weight)


class Links:
    def __init__(self):
        self.shards = lax.axis_size("freq")
        self.fast = self.shards == 2 and lax.axis_size("dp") == 16
        self.place = lax.axis_index("freq")
        index = lax.axis_index("dp")
        self.last = None
        self.core = index % 2
        self.row = (index // 2) % 2
        depth = index // 4
        along = jnp.where(self.row == 0, depth, 7 - depth)
        self.rank = jnp.where(self.core == 0, along, (8 - along) % 8)
        cycle = [z * 4 for z in range(4)] + [z * 4 + 2 for z in range(3, -1, -1)]
        self.ring = []
        for i in range(8):
            self.ring.append((cycle[i], cycle[(i + 1) % 8]))
            self.ring.append((cycle[i] + 1, cycle[(i + 7) % 8] + 1))

    def over_x(self, values):
        return lax.ppermute(values, "freq", [(0, 1), (1, 0)])

    def over_x_in_turn(self, values):
        if self.last is not None:
            values, _ = lax.optimization_barrier((values, self.last))
        self.last = self.over_x(values)
        return self.last

    def over(self, bit, values):
        return lax.ppermute(values, "dp", [(i, i ^ bit) for i in range(16)])

    def over_core(self, values):
        return self.over(1, values)

    def over_ring(self, values):
        return lax.ppermute(values, "dp", self.ring)


def halves(values, which, axis):
    size = values.shape[axis] // 2
    return (
        lax.dynamic_slice_in_dim(values, which * size, size, axis),
        lax.dynamic_slice_in_dim(values, (1 - which) * size, size, axis),
    )


def ordered(which, own, other, axis):
    return jnp.where(
        which == 0,
        jnp.concatenate([own, other], axis),
        jnp.concatenate([other, own], axis),
    )


def fetch_other(links, weight, axis):
    half = halves(weight, links.core, axis)[0]
    quarter = halves(half, links.row, axis)[0]
    quarter = links.over_x_in_turn(quarter)
    half = ordered(links.row, quarter, links.over(2, quarter), axis)
    return jnp.concatenate([half, links.over_core(half)], axis)


def weight_shards(links, weight, axis):
    if links.fast:
        return [weight, fetch_other(links, weight, axis)]
    return [lax.all_gather(weight, "freq", axis=axis, tiled=True)]


def core_sum(links, values, axis):
    keep, send = halves(values, links.core, axis)
    return keep + links.over_core(send)


def quad_sum(links, grads, axis):
    own, across = grads
    size = across.shape[axis] // 2
    keep = lax.slice_in_dim(across, 0, size, axis=axis)
    send = lax.slice_in_dim(across, size, 2 * size, axis=axis)
    across = keep + links.over_core(send)
    return core_sum(links, own, axis) + links.over_x(across)


def ring_kernel(count, *refs):
    parts, sums, others, held = (refs[i * count : (i + 1) * count] for i in range(4))
    out_send, out_recv, back_send, back_recv, core_send, core_recv = refs[4 * count :]
    index, across = lax.axis_index("dp"), lax.axis_index("freq")
    core, row, depth = index % 2, (index // 2) % 2, index // 4
    along = depth * (1 - row) + (7 - depth) * row
    rank = (along * (1 - core) + (8 - along) * core) % 8

    def device(spot):
        spot = spot % 8
        side = spot // 4
        return (spot * (1 - side) + (7 - spot) * side) * 4 + side * 2 + core

    way = 1 - 2 * core
    after, before = (device(along + way + 8), across), (device(along - way + 8), across)
    twin = (index + 1 - 2 * core, across)
    barrier = pltpu.get_barrier_semaphore()
    for partner in (after, before, twin):
        pl.semaphore_signal(barrier, inc=1, device_id=partner, device_id_type=MESH)
    pl.semaphore_wait(barrier, 3)

    def copy(src, dst, send, recv, partner):
        return pltpu.make_async_remote_copy(
            src_ref=src,
            dst_ref=dst,
            send_sem=send,
            recv_sem=recv,
            device_id=partner,
            device_id_type=MESH,
        )

    def outward(i, step, src):
        return copy(src, held[i].at[step], out_send.at[step, i], out_recv.at[step, i], after)

    def backward(i, step, place):
        ref = sums[i].at[place]
        return copy(ref, ref, back_send.at[step, i], back_recv.at[step, i], after)

    def sideward(i, step, place):
        return copy(
            sums[i].at[place],
            others[i].at[place],
            core_send.at[step, i],
            core_recv.at[step, i],
            twin,
        )

    for i in range(count):
        outward(i, 0, parts[i].at[rank]).start()

    def out_step(step, carry):
        place = (rank + 7 - step) % 8
        for i in range(count):
            outward(i, step, held[i].at[step]).wait_recv()
            held[i][step] = held[i][step] + parts[i][place]
            outward(i, step + 1, held[i].at[step]).start()
        return carry

    lax.fori_loop(0, 6, out_step, 0)
    place = (rank + 1) % 8
    for i in range(count):
        outward(i, 6, held[i].at[6]).wait_recv()
        sums[i][place] = held[i][6] + parts[i][place]
        backward(i, 0, place).start()
        sideward(i, 0, place).start()

    def back_step(step, carry):
        place = (rank + 8 - step) % 8
        for i in range(count):
            backward(i, step, place).wait_recv()
            backward(i, step + 1, place).start()
            sideward(i, step + 1, place).start()
        return carry

    lax.fori_loop(0, 6, back_step, 0)
    place = (rank + 2) % 8
    for i in range(count):
        backward(i, 6, place).wait_recv()
        sideward(i, 7, place).start()

    def end_step(step, carry):
        for i in range(count):
            outward(i, step, held[i].at[step]).wait_send()
            backward(i, step, step).wait_send()
            sideward(i, step, step).wait_send()
            sideward(i, step, step).wait_recv()
        return carry

    lax.fori_loop(0, 7, end_step, 0)
    for i in range(count):
        sideward(i, 7, 7).wait_send()
        sideward(i, 7, 7).wait_recv()


def ring_sums(parts, collective_id):
    count = len(parts)
    chunked = [p.reshape((8, p.shape[0] // 8, p.shape[1])) for p in parts]
    shapes = [jax.ShapeDtypeStruct(c.shape, c.dtype) for c in chunked]
    whole = pl.BlockSpec(memory_space=pltpu.VMEM)
    sem = pltpu.SemaphoreType.DMA
    outs = pl.pallas_call(
        lambda *refs: ring_kernel(count, *refs),
        out_shape=shapes * 2,
        in_specs=[whole] * count,
        out_specs=[whole] * (2 * count),
        scratch_shapes=[pltpu.VMEM((7,) + c.shape[1:], c.dtype) for c in chunked]
        + [sem((7, count))] * 4
        + [sem((8, count))] * 2,
        compiler_params=pltpu.CompilerParams(
            collective_id=collective_id, has_side_effects=True, vmem_limit_bytes=VMEM_LIMIT
        ),
        cost_estimate=pl.CostEstimate(
            flops=2 * sum(p.size for p in parts),
            bytes_accessed=6 * sum(p.size for p in parts),
            transcendentals=0,
        ),
    )(*chunked)
    flat = [o.reshape(p.shape) for o, p in zip(outs, parts + parts)]
    return list(zip(flat[:count], flat[count:]))


def column_kernel(sum_rows, core_ref, own_ref, other_ref, out_ref):
    is_own = pl.program_id(1) == core_ref[0]
    filled = pl.program_id(0) < sum_rows

    @pl.when(filled & is_own)
    def _():
        out_ref[...] = own_ref[...].astype(F32)

    @pl.when(filled & ~is_own)
    def _():
        out_ref[...] = other_ref[...].astype(F32)

    @pl.when(~filled)
    def _():
        out_ref[...] = jnp.zeros(out_ref.shape, F32)


def join_columns(links, own, other, rows):
    have, half = own.shape
    block = math.gcd(have, rows)
    block = math.gcd(block, 128)
    have_blocks = have // block
    spec = pl.BlockSpec((block, half), lambda i, j, core: (jnp.minimum(i, have_blocks - 1), 0))
    return pl.pallas_call(
        lambda *refs: column_kernel(have_blocks, *refs),
        grid_spec=pltpu.PrefetchScalarGridSpec(
            num_scalar_prefetch=1,
            grid=(rows // block, 2),
            in_specs=[spec, spec],
            out_specs=pl.BlockSpec((block, half), lambda i, j, core: (i, j)),
        ),
        out_shape=jax.ShapeDtypeStruct((rows, 2 * half), F32),
        compiler_params=pltpu.CompilerParams(vmem_limit_bytes=VMEM_LIMIT),
        cost_estimate=pl.CostEstimate(
            flops=0, bytes_accessed=4 * have * half + 8 * rows * half, transcendentals=0
        ),
    )(links.core.reshape(1), own, other)


def row_kernel(blocks, core_ref, own_ref, other_ref, out_ref):
    is_own = pl.program_id(0) // blocks == core_ref[0]

    @pl.when(is_own)
    def _():
        out_ref[...] = own_ref[...].astype(F32)

    @pl.when(~is_own)
    def _():
        out_ref[...] = other_ref[...].astype(F32)


def join_rows(links, own, other):
    half, width = own.shape
    block = math.gcd(half, 256)
    blocks = half // block

    def spec(mine):
        def place(i, core):
            here = (i // blocks == core[0]) == mine
            return (jnp.where(here, i % blocks, 0), 0)

        return pl.BlockSpec((block, width), place)

    return pl.pallas_call(
        lambda *refs: row_kernel(blocks, *refs),
        grid_spec=pltpu.PrefetchScalarGridSpec(
            num_scalar_prefetch=1,
            grid=(2 * blocks,),
            in_specs=[spec(True), spec(False)],
            out_specs=pl.BlockSpec((block, width), lambda i, core: (i, 0)),
        ),
        out_shape=jax.ShapeDtypeStruct((2 * half, width), F32),
        compiler_params=pltpu.CompilerParams(vmem_limit_bytes=VMEM_LIMIT),
        cost_estimate=pl.CostEstimate(
            flops=0, bytes_accessed=12 * half * width, transcendentals=0
        ),
    )(links.core.reshape(1), own, other)


def join_qkv(links, own, other):
    total = ordered(links.core, own, other, 1)
    depth = own.shape[0] // 3
    return jnp.stack([total[i * depth : (i + 1) * depth] for i in range(3)], axis=1).astype(F32)


def sum_small(links, values):
    if links.fast:
        values = values + links.over_x(values)
        for bit in (1, 2, 4, 8):
            values = values + links.over(bit, values)
        return values
    return lax.psum(values, ("dp", "freq"))


def own_images(links, values):
    count = values.shape[0] // links.shards
    return lax.dynamic_slice_in_dim(values, links.place * count, count, 0)


def reduce_rows(links, partial):
    if links.fast:
        keep, send = halves(partial, links.place, 0)
        return keep + links.over_x_in_turn(send.astype(BF16)).astype(F32)
    return lax.psum_scatter(
        partial.astype(BF16), "freq", scatter_dimension=0, tiled=True
    ).astype(F32)


def gather_rows(links, values):
    if links.fast:
        return ordered(links.place, values, links.over_x(values), 0)
    return lax.all_gather(values, "freq", axis=0, tiled=True)


def block_forward(stream, gains, biases, shards, counts, seq, head_size, masked):
    normed = layer_norm(stream, gains[0], biases[0])
    middle = stream
    heads = []
    for weight_qkv, weight_out, _, _ in shards:
        queries = (dot(normed, weight_qkv[0]) * head_size ** (-0.5)).astype(BF16)
        keys = dot(normed, weight_qkv[1]).astype(BF16)
        values = dot(normed, weight_qkv[2]).astype(BF16)
        mixed = attend(queries, keys, values, counts, seq, head_size, masked)
        middle = middle + dot(mixed, weight_out)
        heads.append((queries, keys, values, mixed))
    normed_mid = layer_norm(middle, gains[1], biases[1])
    result = middle
    units = []
    for _, _, weight_up, weight_down in shards:
        active, slope = up_projection(normed_mid, weight_up)
        result = result + dot(active, weight_down)
        units.append((active, slope))
    return result, (stream, normed, heads, middle, normed_mid, units)


def block_backward(grad, gains, shards, counts, seq, head_size, masked, saved):
    stream, normed, heads, middle, normed_mid, units = saved
    low = grad.astype(BF16)
    down_grads, up_grads, grad_normed = [], [], 0.0
    for (_, _, weight_up, weight_down), (active, slope) in zip(shards, units):
        grad_pre = (dot_nt(low, weight_down) * slope.astype(F32)).astype(BF16)
        grad_normed = grad_normed + dot_nt(grad_pre, weight_up)
        down_grads.append(dot_tn(active, low).astype(BF16))
        up_grads.append(dot_tn(normed_mid, grad_pre).astype(BF16))
    grad_in, mid_gain, mid_bias = layer_norm_back(grad_normed, middle, gains[1])
    grad = grad + grad_in
    low = grad.astype(BF16)
    out_grads, qkv_grads, grad_normed = [], [], 0.0
    for (weight_qkv, weight_out, _, _), (queries, keys, values, mixed) in zip(shards, heads):
        grad_mixed = dot_nt(low, weight_out).astype(BF16)
        grads = attend_back(queries, keys, values, grad_mixed, counts, seq, head_size, masked)
        for i in range(3):
            grad_normed = grad_normed + dot_nt(grads[i], weight_qkv[i])
        out_grads.append(dot_tn(mixed, low).astype(BF16))
        qkv_grads.append([dot_tn(normed, grads[i]).astype(BF16) for i in range(3)])
    grad_in, first_gain, first_bias = layer_norm_back(grad_normed, stream, gains[0])
    return (
        grad + grad_in,
        (first_gain, mid_gain),
        (first_bias, mid_bias),
        (qkv_grads, out_grads, up_grads, down_grads),
    )


def local(
    pixels,
    band_group,
    mask_order,
    visible_count,
    scale_id,
    patch_weight,
    enc_qkv,
    enc_out,
    enc_up,
    enc_down,
    enc_gains,
    enc_biases,
    dec_embed,
    mask_token,
    dec_qkv,
    dec_out,
    dec_up,
    dec_down,
    dec_gains,
    dec_biases,
    head_weight,
    recon_cotangent,
):
    links = Links()
    images, _, pixel_width = pixels.shape
    own = images // links.shards
    own_slots = own * VIS
    rgb_width = min(RGB_PIX, pixel_width)

    stacked = lambda weight: jnp.stack([weight[:, i] for i in range(3)])
    enc_parts = [weight_shards(links, stacked(enc_qkv), 2), weight_shards(links, enc_out, 0)]

    slot_ids = mask_order[:, :VIS]
    one_hot = slot_ids[:, :, None] == jnp.arange(NPATCH)[None, None, :]
    picked = jnp.einsum(
        "bsp,bpc->bsc", one_hot.astype(BF16), pixels, preferred_element_type=F32
    ).astype(BF16)
    multi = (band_group == 0)[:, None, None]
    zero = jnp.zeros((), BF16)
    rgb_valid = links.place * pixel_width + jnp.arange(rgb_width) < RGB_PIX
    picked_multi = jnp.where(multi, picked, zero).reshape(images * VIS, pixel_width)
    picked_rgb = jnp.where(~multi & rgb_valid, picked[:, :, :rgb_width], zero)
    picked_rgb = picked_rgb.reshape(images * VIS, rgb_width)
    patch_rgb = patch_weight[1, :rgb_width]
    partial = dot(picked_multi, patch_weight[0]) + dot(picked_rgb, patch_rgb)
    embedded = reduce_rows(links, partial)
    enc_parts += [weight_shards(links, enc_up, 1), weight_shards(links, enc_down, 0)]
    enc_shards = list(zip(*enc_parts))
    dec_parts = [
        weight_shards(links, stacked(dec_qkv), 2),
        weight_shards(links, dec_out, 0),
        weight_shards(links, dec_up, 1),
        weight_shards(links, dec_down, 0),
    ]
    dec_shards = list(zip(*dec_parts))
    cotangent = recon_cotangent.reshape(images * NPATCH, -1)
    grad_final = reduce_rows(links, dot_nt(cotangent, head_weight))

    my_slots = own_images(links, slot_ids)
    my_count = own_images(links, visible_count)
    ratios = jnp.exp2(own_images(links, scale_id).astype(F32) - 1.0)
    stream = embedded + slot_codes(my_slots, ratios, D).reshape(own_slots, D)

    stream, enc_saved = block_forward(
        stream, enc_gains, enc_biases, enc_shards, my_count, VIS, HDIM, True
    )
    latent = layer_norm(stream, enc_gains[2], enc_biases[2])
    lifted = dot(latent, dec_embed)

    live = jnp.arange(VIS)[None, :] < my_count[:, None]
    select = (my_slots[:, :, None] == jnp.arange(NPATCH)[None, None, :]) & live[:, :, None]
    hidden = 1.0 - jnp.sum(select.astype(F32), axis=1)[:, :, None]
    decoded = (
        jnp.einsum(
            "bsp,bse->bpe",
            select.astype(F32),
            lifted.reshape(own, VIS, DDEC),
            precision=HIGHEST,
        )
        + hidden * mask_token
        + grid_codes(ratios, DDEC)
    ).reshape(own * NPATCH, DDEC)
    decoded, dec_saved = block_forward(
        decoded, dec_gains, dec_biases, dec_shards, my_count, NPATCH, DHDIM, False
    )
    final_own = layer_norm(decoded, dec_gains[2], dec_biases[2])

    final_all = gather_rows(links, final_own)
    reconstructions = dot(final_all, head_weight).astype(BF16).reshape(images, NPATCH, -1)
    head_grad = dot_tn(final_all, cotangent).astype(BF16)

    grad_in, dec_gain_2, dec_bias_2 = layer_norm_back(grad_final, decoded, dec_gains[2])
    grad_decoded, dec_gain_01, dec_bias_01, dec_grads = block_backward(
        grad_in, dec_gains, dec_shards, my_count, NPATCH, DHDIM, False, dec_saved
    )
    grad_grid = grad_decoded.reshape(own, NPATCH, DDEC)
    mask_grad = jnp.sum(hidden * grad_grid, axis=(0, 1))
    grad_lifted = (
        jnp.einsum(
            "bsp,bpe->bse",
            select.astype(BF16),
            grad_grid.astype(BF16),
            preferred_element_type=F32,
        )
        .astype(BF16)
        .reshape(own_slots, DDEC)
    )
    embed_grad = dot_tn(latent, grad_lifted).astype(BF16)
    grad_latent = dot_nt(grad_lifted, dec_embed)

    grad_in, enc_gain_2, enc_bias_2 = layer_norm_back(grad_latent, stream, enc_gains[2])
    grad_stream, enc_gain_01, enc_bias_01, enc_grads = block_backward(
        grad_in, enc_gains, enc_shards, my_count, VIS, HDIM, True, enc_saved
    )

    grad_embedded = gather_rows(links, grad_stream.astype(BF16))
    patch_grads = [
        dot_tn(picked_multi, grad_embedded).astype(BF16),
        dot_tn(picked_rgb, grad_embedded).astype(BF16),
    ]
    multi_rows = jnp.repeat(band_group == 0, VIS)[:, None]
    back_multi = dot_nt(jnp.where(multi_rows, grad_embedded, zero), patch_weight[0])
    back_rgb = dot_nt(jnp.where(multi_rows, zero, grad_embedded), patch_rgb)
    back_rgb = jnp.where(rgb_valid, back_rgb, 0.0)
    back = back_multi + jnp.pad(back_rgb, ((0, 0), (0, pixel_width - rgb_width)))
    pixel_grad = jnp.einsum(
        "bsp,bsc->bpc",
        one_hot.astype(BF16),
        back.astype(BF16).reshape(images, VIS, pixel_width),
        preferred_element_type=F32,
    )

    dec_qkv_grads, dec_out_grads, dec_up_grads, dec_down_grads = dec_grads
    enc_qkv_grads, enc_out_grads, enc_up_grads, enc_down_grads = enc_grads
    stacked_qkv = lambda grads: [jnp.concatenate(g, 0) for g in grads]
    enc_stack = [
        (stacked_qkv(enc_qkv_grads), 1),
        (enc_out_grads, 0),
        (enc_up_grads, 1),
        (enc_down_grads, 0),
    ]
    dec_stack = [
        (stacked_qkv(dec_qkv_grads), 1),
        (dec_out_grads, 0),
        (dec_up_grads, 1),
        (dec_down_grads, 0),
    ]
    patch_grad = jnp.concatenate(patch_grads, 0)
    if links.fast:
        early = [quad_sum(links, g, axis) for g, axis in dec_stack]
        embed_part = core_sum(links, embed_grad, 0)
        early += [embed_part + links.over_x(embed_part), core_sum(links, head_grad, 1)]
        late = [quad_sum(links, g, axis) for g, axis in enc_stack]
        late += [core_sum(links, patch_grad, 1)]
        early = ring_sums(early, 1)
        late = ring_sums(late, 2)
        totals = []
        for group in (early, late):
            totals.append(
                [
                    join_qkv(links, *group[0]),
                    join_rows(links, *group[1]),
                    join_columns(links, *group[2], group[2][0].shape[0]),
                    join_rows(links, *group[3]),
                ]
            )
        dec_totals, enc_totals = totals
        embed_total = join_rows(links, *early[4])
        head_total = join_columns(links, *early[5], DDEC)
        patch_total = join_columns(links, *late[4], 2 * pixel_width)
        patch_total = patch_total.reshape(2, pixel_width, D)
    else:
        reduced = []
        for stack, depth in ((dec_stack, DDEC), (enc_stack, D)):
            parts = [
                lax.psum_scatter(g[0], "freq", scatter_dimension=axis, tiled=True)
                for g, axis in stack
            ]
            parts = [lax.psum(part, "dp").astype(F32) for part in parts]
            parts[0] = jnp.stack(
                [parts[0][i * depth : (i + 1) * depth] for i in range(3)], axis=1
            )
            reduced.append(parts)
        dec_totals, enc_totals = reduced
        embed_total = lax.psum(embed_grad, ("dp", "freq")).astype(F32)
        head_total = lax.psum(head_grad, "dp").astype(F32)
        patch_sum = lax.psum(patch_grad, "dp").astype(F32)
        patch_total = jnp.stack(
            [
                patch_sum[:pixel_width],
                jnp.pad(patch_sum[pixel_width:], ((0, pixel_width - rgb_width), (0, 0))),
            ]
        )
    small = [*enc_gain_01, enc_gain_2, *enc_bias_01, enc_bias_2]
    small += [*dec_gain_01, dec_gain_2, *dec_bias_01, dec_bias_2, mask_grad]
    small = sum_small(links, jnp.concatenate(small).reshape(-1, LANES)).reshape(-1)
    enc_end, dec_end = 6 * D, 6 * D + 6 * DDEC
    enc_small = small[:enc_end].reshape(2, 3, D)
    dec_small = small[enc_end:dec_end].reshape(2, 3, DDEC)
    return (
        reconstructions,
        pixel_grad,
        patch_total,
        *enc_totals,
        enc_small[0],
        enc_small[1],
        embed_total,
        small[dec_end:],
        *dec_totals,
        dec_small[0],
        dec_small[1],
        head_total,
    )


def solution(mesh):
    return jax.shard_map(
        local,
        mesh=mesh,
        in_specs=(
            P("dp", None, "freq"),
            P("dp"),
            P("dp", None),
            P("dp"),
            P("dp"),
            P(None, "freq", None),
            P(None, None, "freq"),
            P("freq", None),
            P(None, "freq"),
            P("freq", None),
            P(),
            P(),
            P(),
            P(),
            P(None, None, "freq"),
            P("freq", None),
            P(None, "freq"),
            P("freq", None),
            P(),
            P(),
            P(None, "freq"),
            P("dp", None, "freq"),
        ),
        out_specs=(
            P("dp", None, "freq"),
            P("dp", None, "freq"),
            P(None, "freq", None),
            P(None, None, "freq"),
            P("freq", None),
            P(None, "freq"),
            P("freq", None),
            P(),
            P(),
            P(),
            P(),
            P(None, None, "freq"),
            P("freq", None),
            P(None, "freq"),
            P("freq", None),
            P(),
            P(),
            P(None, "freq"),
        ),
        check_vma=False,
    )
```

```python
import math

import jax
import jax.numpy as jnp
from jax import lax
from jax.experimental import pallas as pl
from jax.experimental.pallas import tpu as pltpu
from jax.sharding import PartitionSpec as P

D = 1024
HDIM = 64
DDEC = 512
DHDIM = 32
RGB_PIX = 768
SIDE = 16
NPATCH = 256
VIS = 64

HIGHEST = lax.Precision.HIGHEST
EPSILON = 1e-06
MASKED = -1e30
BF16 = jnp.bfloat16
F32 = jnp.float32
LANES = 128
VMEM_LIMIT = 48 * 1024 * 1024
RING_VMEM_LIMIT = 58 * 1024 * 1024
MESH = pl.DeviceIdType.MESH


def dot(left, right):
    return jnp.dot(left, right, preferred_element_type=F32)


def dot_tn(left, right):
    return lax.dot_general(left, right, (((0,), (0,)), ((), ())), preferred_element_type=F32)


def dot_nt(left, right):
    return lax.dot_general(left, right, (((1,), (1,)), ((), ())), preferred_element_type=F32)


def normalize(values):
    center = values - jnp.mean(values, -1, keepdims=True)
    rstd = lax.rsqrt(jnp.mean(center * center, -1, keepdims=True) + EPSILON)
    return center * rstd, rstd


def layer_norm(values, scales, shifts):
    return (normalize(values)[0] * scales + shifts).astype(BF16)


def layer_norm_back(grad, values, scales):
    unit, rstd = normalize(values)
    scaled = grad * scales
    mean_grad = jnp.mean(scaled, -1, keepdims=True)
    mean_along = jnp.mean(scaled * unit, -1, keepdims=True)
    grad_in = rstd * (scaled - mean_grad - unit * mean_along)
    return grad_in, jnp.sum(grad * unit, 0), jnp.sum(grad, 0)


def code_tables(ratios, features):
    quarter = features // 4
    index_f = jnp.arange(quarter, dtype=F32)
    frequencies = jnp.exp(index_f * (-math.log(10000.0) / quarter))
    places = jnp.arange(SIDE).astype(F32)
    angle = (places[None, :] * ratios[:, None])[..., None] * frequencies
    return jnp.concatenate([jnp.sin(angle), jnp.cos(angle)], -1)


def slot_codes(slot_ids, ratios, features):
    table = code_tables(ratios, features)
    places = jnp.arange(SIDE)
    row = (slot_ids[..., None] // SIDE == places).astype(F32)
    col = (slot_ids[..., None] % SIDE == places).astype(F32)
    pick = lambda one_hot: jnp.einsum("bsp,bpf->bsf", one_hot, table, precision=HIGHEST)
    return jnp.concatenate([pick(row), pick(col)], -1)


def grid_codes(ratios, features):
    table = code_tables(ratios, features)
    images, _, half = table.shape
    row = jnp.broadcast_to(table[:, :, None, :], (images, SIDE, SIDE, half))
    col = jnp.broadcast_to(table[:, None, :, :], (images, SIDE, SIDE, half))
    return jnp.concatenate([row, col], -1).reshape(images, NPATCH, features)


def head_rows(values, head_size, heads):
    lane = lax.broadcasted_iota(jnp.int32, (1, LANES), 1)
    return jnp.concatenate(
        [jnp.where(lane // head_size == h, values, 0).astype(BF16) for h in heads], 0
    )


def head_parts(values, head_size, seq, merge):
    return [
        values[j * head_size : (j + 1) * head_size, j * seq : (j + 1) * seq] for j in range(merge)
    ]


def masked_scores(keys, queries, valid):
    scores = dot_nt(keys, queries)
    if valid is not None:
        scores = jnp.where(valid > 0.0, scores, MASKED)
    return scores


def attend_rows(head_size, merge, q_ref, k_ref, v_ref, o_ref, valid):
    seq, width = q_ref.shape
    for g in range(width // LANES):
        lanes = slice(g * LANES, (g + 1) * LANES)
        queries, keys, values = q_ref[:, lanes], k_ref[:, lanes], v_ref[:, lanes]
        values_t = jnp.transpose(values)
        parts = []
        for h in range(0, LANES // head_size, merge):
            scores = masked_scores(
                keys, head_rows(queries, head_size, range(h, h + merge)), valid
            )
            top = jnp.max(scores, 0, keepdims=True)
            power = jnp.exp(scores - top)
            total = jnp.sum(power, 0, keepdims=True)
            rows = slice(h * head_size, (h + merge) * head_size)
            mixed = dot(values_t[rows], power.astype(BF16)) * (1.0 / total)
            parts += head_parts(mixed, head_size, seq, merge)
        o_ref[:, lanes] = jnp.transpose(jnp.concatenate(parts, 0)).astype(BF16)


def attend_back_rows(
    head_size, merge, q_ref, k_ref, v_ref, g_ref, dq_ref, dk_ref, dv_ref, valid
):
    seq, width = q_ref.shape
    factor = head_size ** (-0.5)
    for g in range(width // LANES):
        lanes = slice(g * LANES, (g + 1) * LANES)
        queries, keys, values, grads = (
            q_ref[:, lanes],
            k_ref[:, lanes],
            v_ref[:, lanes],
            g_ref[:, lanes],
        )
        keys_t = jnp.transpose(keys)
        parts, dk_sum, dv_sum = [], 0.0, 0.0
        for h in range(0, LANES // head_size, merge):
            own_q = head_rows(queries, head_size, range(h, h + merge))
            own_g = head_rows(grads, head_size, range(h, h + merge))
            scores = masked_scores(keys, own_q, valid)
            top = jnp.max(scores, 0, keepdims=True)
            power = jnp.exp(scores - top)
            weights = power * (1.0 / jnp.sum(power, 0, keepdims=True))
            dv_sum += dot(weights.astype(BF16), own_g)
            grad_weights = dot_nt(values, own_g)
            along = jnp.sum(weights * grad_weights, 0, keepdims=True)
            grad_scores = (weights * (grad_weights - along)).astype(BF16)
            dk_sum += dot(grad_scores, own_q)
            rows = slice(h * head_size, (h + merge) * head_size)
            grad_q = dot(keys_t[rows], grad_scores) * factor
            parts += head_parts(grad_q, head_size, seq, merge)
        dq_ref[:, lanes] = jnp.transpose(jnp.concatenate(parts, 0)).astype(BF16)
        dk_ref[:, lanes] = dk_sum.astype(BF16)
        dv_ref[:, lanes] = dv_sum.astype(BF16)


def valid_rows(counts, seq, merge):
    valid = (jnp.arange(seq)[None, :, None] < counts[:, None, None]).astype(F32)
    return jnp.broadcast_to(valid, (counts.shape[0], seq, merge * seq))


def attention_call(rows_fn, arrays, valid, seq, n_out, head_size, merge, flop_factor):
    rows, width = arrays[0].shape
    images = rows // seq
    block = pl.BlockSpec((seq, width), lambda i: (i, 0))
    out = jax.ShapeDtypeStruct((rows, width), BF16)
    in_specs, masks = [block] * len(arrays), []
    if valid is not None:
        in_specs.append(pl.BlockSpec((None,) + valid.shape[1:], lambda i: (i, 0, 0)))
        masks = [valid]

    def kernel(*refs):
        refs = list(refs)
        mask = refs.pop(len(arrays))[...] if masks else None
        rows_fn(head_size, merge, *refs, mask)

    return pl.pallas_call(
        kernel,
        grid=(images,),
        in_specs=in_specs,
        out_specs=[block] * n_out,
        out_shape=[out] * n_out,
        compiler_params=pltpu.CompilerParams(vmem_limit_bytes=VMEM_LIMIT),
        cost_estimate=pl.CostEstimate(
            flops=flop_factor * rows * seq * width * (LANES // head_size),
            bytes_accessed=(len(arrays) + n_out) * rows * width * 2,
            transcendentals=rows * seq * width // head_size,
        ),
    )(*arrays, *masks)


def attend(queries, keys, values, counts, seq, head_size, masked):
    merge = LANES // head_size
    valid = valid_rows(counts, seq, merge) if masked else None
    arrays = [queries, keys, values]
    return attention_call(attend_rows, arrays, valid, seq, 1, head_size, merge, 4)[0]


def attend_back(queries, keys, values, grads, counts, seq, head_size, masked):
    merge = 1 if masked else LANES // head_size
    valid = valid_rows(counts, seq, merge) if masked else None
    arrays = [queries, keys, values, grads]
    return attention_call(attend_back_rows, arrays, valid, seq, 3, head_size, merge, 10)


def up_kernel(x_ref, w_ref, active_ref, slope_ref):
    pre = dot(x_ref[...], w_ref[...])
    cdf = 0.5 + 0.5 * lax.erf(pre * math.sqrt(0.5))
    density = jnp.exp(-0.5 * pre * pre) * (1.0 / math.sqrt(2.0 * math.pi))
    active_ref[...] = (pre * cdf).astype(BF16)
    slope_ref[...] = (cdf + pre * density).astype(BF16)


def up_projection(rows_in, weight):
    rows, depth = rows_in.shape
    width = weight.shape[1]
    row_block = math.gcd(rows, 512)
    col_block = math.gcd(width, 512)
    out = jax.ShapeDtypeStruct((rows, width), BF16)
    spec = pl.BlockSpec((row_block, col_block), lambda i, j: (i, j))
    return pl.pallas_call(
        up_kernel,
        grid=(rows // row_block, width // col_block),
        in_specs=[
            pl.BlockSpec((row_block, depth), lambda i, j: (i, 0)),
            pl.BlockSpec((depth, col_block), lambda i, j: (0, j)),
        ],
        out_specs=[spec, spec],
        out_shape=[out, out],
        compiler_params=pltpu.CompilerParams(vmem_limit_bytes=VMEM_LIMIT),
        cost_estimate=pl.CostEstimate(
            flops=2 * rows * depth * width,
            bytes_accessed=2 * (rows * depth + depth * width + 2 * rows * width),
            transcendentals=2 * rows * width,
        ),
    )(rows_in, weight)


class Links:
    def __init__(self):
        self.shards = lax.axis_size("freq")
        self.fast = self.shards == 2 and lax.axis_size("dp") == 16
        self.place = lax.axis_index("freq")
        index = lax.axis_index("dp")
        self.core = index % 2
        self.row = (index // 2) % 2
        depth = index // 4
        along = jnp.where(self.row == 0, depth, 7 - depth)
        self.rank = jnp.where(self.core == 0, along, (8 - along) % 8)
        cycle = [z * 4 for z in range(4)] + [z * 4 + 2 for z in range(3, -1, -1)]
        self.ring = []
        for i in range(8):
            self.ring.append((cycle[i], cycle[(i + 1) % 8]))
            self.ring.append((cycle[i] + 1, cycle[(i + 7) % 8] + 1))

    def over_x(self, values):
        return lax.ppermute(values, "freq", [(0, 1), (1, 0)])

    def over(self, bit, values):
        return lax.ppermute(values, "dp", [(i, i ^ bit) for i in range(16)])

    def over_core(self, values):
        return self.over(1, values)

    def over_ring(self, values):
        return lax.ppermute(values, "dp", self.ring)


def halves(values, which, axis):
    size = values.shape[axis] // 2
    return (
        lax.dynamic_slice_in_dim(values, which * size, size, axis),
        lax.dynamic_slice_in_dim(values, (1 - which) * size, size, axis),
    )


def ordered(which, own, other, axis):
    return jnp.where(
        which == 0,
        jnp.concatenate([own, other], axis),
        jnp.concatenate([other, own], axis),
    )


class Fetch:
    STEPS = 4

    def __init__(self, sources, targets, send, recv):
        self.sources, self.targets, self.send, self.recv = sources, targets, send, recv
        index, across = lax.axis_index("dp"), lax.axis_index("freq")
        core, row = index % 2, (index // 2) % 2
        self.quarter = index % 4
        self.next_quarter = self.quarter + 2 - 4 * row
        self.facing = (index, 1 - across)
        self.beside = (index + 2 - 4 * row, across)
        self.twin = (index + 1 - 2 * core, across)

    def greet(self):
        barrier = pltpu.get_barrier_semaphore()
        for partner in (self.facing, self.beside, self.twin):
            pl.semaphore_signal(barrier, inc=1, device_id=partner, device_id_type=MESH)
        pl.semaphore_wait(barrier, 3)

    def view(self, ref, quarter):
        rows = ref.shape[-2] // 4
        place = pl.ds(pl.multiple_of(quarter * rows, 16), rows)
        return ref.at[:, place] if len(ref.shape) == 3 else ref.at[place]

    def copy(self, i, step):
        quarter = self.next_quarter if step == 3 else self.quarter
        target = self.view(self.targets[i], quarter)
        return pltpu.make_async_remote_copy(
            src_ref=self.view(self.sources[i], quarter) if step == 0 else target,
            dst_ref=target,
            send_sem=self.send.at[step, i],
            recv_sem=self.recv.at[step, i],
            device_id=(self.facing, self.beside, self.twin, self.twin)[step],
            device_id_type=MESH,
        )

    def start(self, items):
        for i in items:
            self.copy(i, 0).start()

    def pass_on(self, items):
        for i in items:
            self.copy(i, 0).wait_recv()
            self.copy(i, 1).start()
            self.copy(i, 2).start()

    def pass_on_last(self, items):
        for i in items:
            self.copy(i, 1).wait_recv()
            self.copy(i, 3).start()

    def finish(self):
        for i in range(len(self.sources)):
            for step in range(self.STEPS):
                self.copy(i, step).wait_send()
                if step >= 2:
                    self.copy(i, step).wait_recv()


def head_start_kernel(rows_ref, qkv_ref, out_ref, cot_ref, head_ref, *refs):
    got_ref, new_qkv, new_out, partial_ref, tiles, sums = refs[:6]
    send, recv, row_send, row_recv, tile_sem, sum_sem = refs[6:]
    fetch = Fetch([qkv_ref, out_ref], [new_qkv, new_out], send, recv)
    fetch.greet()
    rows_copy = pltpu.make_async_remote_copy(
        src_ref=rows_ref,
        dst_ref=got_ref,
        send_sem=row_send,
        recv_sem=row_recv,
        device_id=fetch.facing,
        device_id_type=MESH,
    )
    fetch.start([0, 1])
    tile = tiles.shape[1]
    count = cot_ref.shape[0] // tile

    def load(i, slot):
        return pltpu.make_async_copy(
            cot_ref.at[pl.ds(i * tile, tile)], tiles.at[slot], tile_sem.at[slot]
        )

    def store(i, slot):
        return pltpu.make_async_copy(
            sums.at[slot], partial_ref.at[pl.ds(i * tile, tile)], sum_sem.at[slot]
        )

    load(0, 0).start()
    load(1, 1).start()

    def body(pair, carry):
        for slot in range(2):
            i = pair * 2 + slot
            load(i, slot).wait()

            @pl.when(pair > 0)
            def _():
                store(i - 2, slot).wait()

            sums[slot] = dot_nt(tiles[slot], head_ref[...]).astype(BF16)
            store(i, slot).start()

            @pl.when(pair < count // 2 - 1)
            def _():
                load(i + 2, slot).start()

        return carry

    lax.fori_loop(0, count // 2, body, 0)
    for slot in range(2):
        store(count - 2 + slot, slot).wait()
    fetch.pass_on([0, 1])
    rows_copy.start()
    fetch.pass_on_last([0, 1])
    fetch.finish()
    rows_copy.wait()


def head_start(rows, weight_qkv, weight_out, cotangent, head_weight):
    hbm, vmem = pl.BlockSpec(memory_space=pl.ANY), pl.BlockSpec(memory_space=pltpu.VMEM)
    sem, shape = pltpu.SemaphoreType.DMA, lambda a: jax.ShapeDtypeStruct(a.shape, a.dtype)
    count, columns = cotangent.shape
    width = head_weight.shape[0]
    tile = 256
    return pl.pallas_call(
        head_start_kernel,
        out_shape=[
            shape(rows),
            shape(weight_qkv),
            shape(weight_out),
            jax.ShapeDtypeStruct((count, width), BF16),
        ],
        in_specs=[hbm] * 4 + [vmem],
        out_specs=[hbm] * 4,
        scratch_shapes=[
            pltpu.VMEM((2, tile, columns), BF16),
            pltpu.VMEM((2, tile, width), BF16),
            sem((4, 2)),
            sem((4, 2)),
            sem,
            sem,
            sem((2,)),
            sem((2,)),
        ],
        compiler_params=pltpu.CompilerParams(
            collective_id=2, has_side_effects=True, vmem_limit_bytes=VMEM_LIMIT
        ),
        cost_estimate=pl.CostEstimate(
            flops=2 * count * columns * width,
            bytes_accessed=2 * count * columns,
            transcendentals=0,
        ),
    )(rows, weight_qkv, weight_out, cotangent, head_weight)


def attend_fetch_kernel(head_size, merge, steps, *refs):
    own, other, valid_ref, sources = refs[:3], refs[3:6], refs[6], refs[7:13]
    own_out, other_out, targets = refs[13], refs[14], refs[15:21]
    send, recv = refs[21:]
    fetch = Fetch(sources, targets, send, recv)

    @pl.when(pl.program_id(0) == 0)
    def _():
        fetch.greet()
        fetch.start([0])

    valid = valid_ref[...]
    attend_rows(head_size, merge, *own, own_out, valid)
    attend_rows(head_size, merge, *other, other_out, valid)

    @pl.when(pl.program_id(0) == steps - 1)
    def _():
        rest = list(range(2, 6))
        fetch.pass_on([0])
        fetch.start([1])
        fetch.pass_on([1])
        fetch.start(rest)
        fetch.pass_on_last([0, 1])
        fetch.pass_on(rest)
        fetch.pass_on_last(rest)
        fetch.finish()


def attend_fetch(own, other, counts, seq, head_size, weights):
    rows, width = own[0].shape
    images, merge = rows // seq, LANES // head_size
    block = pl.BlockSpec((seq, width), lambda i: (i, 0))
    hbm, sem = pl.BlockSpec(memory_space=pl.ANY), pltpu.SemaphoreType.DMA
    valid = valid_rows(counts, seq, merge)
    out = jax.ShapeDtypeStruct((rows, width), BF16)
    return pl.pallas_call(
        lambda *refs: attend_fetch_kernel(head_size, merge, images, *refs),
        grid=(images,),
        out_shape=[out, out] + [jax.ShapeDtypeStruct(w.shape, w.dtype) for w in weights],
        in_specs=[block] * 6
        + [pl.BlockSpec((None,) + valid.shape[1:], lambda i: (i, 0, 0))]
        + [hbm] * len(weights),
        out_specs=[block] * 2 + [hbm] * len(weights),
        scratch_shapes=[sem((4, len(weights)))] * 2,
        compiler_params=pltpu.CompilerParams(
            collective_id=3, has_side_effects=True, vmem_limit_bytes=VMEM_LIMIT
        ),
        cost_estimate=pl.CostEstimate(
            flops=8 * rows * seq * width * merge,
            bytes_accessed=16 * rows * width,
            transcendentals=2 * rows * seq * width // head_size,
        ),
    )(*own, *other, valid, *weights)


def whole_weight(weight, axis):
    return lax.all_gather(weight, "freq", axis=axis, tiled=True)


def core_sum(links, values, axis):
    keep, send = halves(values, links.core, axis)
    return keep + links.over_core(send)


def ring_kernel(shapes, crossing, pairs, *refs):
    count = len(shapes) - len(pairs)
    total = len(shapes)
    every = total + crossing

    def take(number):
        nonlocal refs
        head, refs = refs[:number], refs[number:]
        return head

    arrays, sums = take(every), take(count)
    mine, twins = take(every), take(every)
    held, crossed, first, done = take(total), take(crossing), take(crossing), take(total)
    arrived = take(len(pairs))
    out_send, out_recv, back_send, back_recv, side_send, side_recv, own_sem = take(7)
    x_send, x_recv, end_send, end_recv, load_sem, core_send, core_recv = take(7)
    index, across = lax.axis_index("dp"), lax.axis_index("freq")
    core, row, depth = index % 2, (index // 2) % 2, index // 4
    along = depth * (1 - row) + (7 - depth) * row
    rank = (along * (1 - core) + (8 - along) * core) % 8
    twin_rank = (8 - rank) % 8

    def device(spot):
        spot = spot % 8
        side = spot // 4
        return (spot * (1 - side) + (7 - spot) * side) * 4 + side * 2 + core

    way = 1 - 2 * core
    after, before = (device(along + way + 8), across), (device(along - way + 8), across)
    twin, facing = (index + 1 - 2 * core, across), (index, 1 - across)
    barrier = pltpu.get_barrier_semaphore()
    for partner in (after, before, twin, facing):
        pl.semaphore_signal(barrier, inc=1, device_id=partner, device_id_type=MESH)
    pl.semaphore_wait(barrier, 4)

    def copy(src, dst, send, recv, partner):
        return pltpu.make_async_remote_copy(
            src_ref=src,
            dst_ref=dst,
            send_sem=send,
            recv_sem=recv,
            device_id=partner,
            device_id_type=MESH,
        )

    def chunk(ref, half, place):
        if ref.shape[0] == 16:
            return ref.at[half * 8 + place]
        width = ref.shape[2] // 2
        return ref.at[place, :, pl.ds(pl.multiple_of(half * width, 128), width)]

    def load(i, step):
        place = (rank + 8 - step) % 8
        return pltpu.make_async_copy(
            chunk(arrays[i], core, place), mine[i].at[step], load_sem.at[step, i]
        )

    def coreward(i, step):
        place = (twin_rank + 8 - step) % 8
        return copy(
            chunk(arrays[i], 1 - core, place),
            twins[i].at[step % 4],
            core_send.at[step, i],
            core_recv.at[step, i],
            twin,
        )

    def core_sum(i, step, more):
        load(i, step).wait()
        coreward(i, step).wait_recv()
        value = mine[i][step] + twins[i][step % 4]
        mine[i][step] = value
        if more:
            coreward(i, step + 2).start()
        return value

    def facingward(i, step):
        return copy(
            mine[total + i].at[step],
            crossed[i].at[step % 4],
            x_send.at[step, i],
            x_recv.at[step, i],
            facing,
        )

    def cross(i, step, more):
        core_sum(total + i, step, more)
        facingward(i, step).start()

    def own(i, step, more, later):
        value = core_sum(i, step, more)
        if i >= crossing:
            return value
        facingward(i, step).wait_recv()
        value = value + crossed[i][step % 4]
        if more:
            mine[i][step] = value
            cross(i, step + 2, later)
        return value

    def outward(i, step, src):
        return copy(src, held[i].at[step], out_send.at[step, i], out_recv.at[step, i], after)

    def backward(i, step, place, src):
        return copy(
            src,
            chunk(sums[i], core, place),
            back_send.at[step, i],
            back_recv.at[step, i],
            after,
        )

    def sideward(i, step, place, src):
        return copy(
            src, chunk(sums[i], core, place), side_send.at[step, i], side_recv.at[step, i], twin
        )

    def keep(i, place):
        return pltpu.make_async_copy(done[i], chunk(sums[i], core, place), own_sem.at[i])

    def lastward(j):
        return copy(done[count + j], arrived[j], end_send.at[j], end_recv.at[j], facing)

    order = list(range(crossing, total)) + list(range(crossing))
    crossers = list(range(total, every))
    for step in range(8):
        for i in crossers + order:
            load(i, step).start()
            if step < 2:
                coreward(i, step).start()
    for step in range(2):
        for i in range(crossing):
            cross(i, step, True)
    for i in order:
        first_ref = mine[i].at[0] if i >= crossing else first[i]
        value = own(i, 0, True, True)
        if i < crossing:
            first[i][...] = value
        outward(i, 0, first_ref).start()

    def out_step(more, later):
        def body(step, carry):
            for i in order:
                outward(i, step, held[i].at[step]).wait_recv()
                held[i][step] = held[i][step] + own(i, step + 1, more, later)
                outward(i, step + 1, held[i].at[step]).start()
            return carry

        return body

    lax.fori_loop(0, 3, out_step(True, True), 0)
    lax.fori_loop(3, 5, out_step(True, False), 0)
    lax.fori_loop(5, 6, out_step(False, False), 0)
    place = (rank + 1) % 8
    for i in range(count, total):
        outward(i, 6, held[i].at[6]).wait_recv()
        done[i][...] = held[i][6] + own(i, 7, False, False)
        lastward(i - count).start()
    for i in order:
        if i >= count:
            continue
        outward(i, 6, held[i].at[6]).wait_recv()
        value = held[i][6] + own(i, 7, False, False)
        if i in pairs:
            lastward(pairs.index(i)).wait_recv()
            value = value + arrived[pairs.index(i)][...]
        done[i][...] = value
        backward(i, 0, place, done[i]).start()
        sideward(i, 0, place, done[i]).start()
        keep(i, place).start()

    def back_step(step, carry):
        place = (rank + 8 - step) % 8
        for i in range(count):
            ref = chunk(sums[i], core, place)
            backward(i, step, place, ref).wait_recv()
            backward(i, step + 1, place, ref).start()
            sideward(i, step + 1, place, ref).start()
        return carry

    lax.fori_loop(0, 6, back_step, 0)
    place = (rank + 2) % 8
    for i in range(count):
        ref = chunk(sums[i], core, place)
        backward(i, 6, place, ref).wait_recv()
        sideward(i, 7, place, ref).start()

    def end_step(step, carry):
        for i in range(total):
            outward(i, step, held[i].at[step]).wait_send()
        for i in range(count):
            backward(i, step, step, chunk(sums[i], core, step)).wait_send()
            sideward(i, step, step, chunk(sums[i], core, step)).wait_send()
            sideward(i, step, step, chunk(sums[i], core, step)).wait_recv()
        for i in range(crossing):
            facingward(i, step).wait_send()
        for i in range(every):
            coreward(i, step).wait_send()
        return carry

    lax.fori_loop(0, 7, end_step, 0)
    for i in range(count):
        sideward(i, 7, 7, chunk(sums[i], core, 7)).wait_send()
        sideward(i, 7, 7, chunk(sums[i], core, 7)).wait_recv()
        keep(i, 7).wait()
    for i in range(crossing):
        facingward(i, 7).wait_send()
    for i in range(every):
        coreward(i, 7).wait_send()
    for j in range(len(pairs)):
        lastward(j).wait_send()


def ring_sums(grads, cross, extra, columns):
    count, crossing, pairs = len(grads), len(cross), sorted(extra)
    total = count + len(pairs)
    arrays = []
    for i, grad in enumerate(list(grads) + [extra[i] for i in pairs] + list(cross)):
        pieces = 8 if i in columns else 16
        arrays.append(grad.reshape(pieces, grad.shape[0] // pieces, grad.shape[1]))
    shapes = [
        (a.shape[1], a.shape[2] // 2 if i in columns else a.shape[2])
        for i, a in enumerate(arrays)
    ]
    hbm, sem = pl.BlockSpec(memory_space=pl.ANY), pltpu.SemaphoreType.DMA
    slots = lambda number, of: [pltpu.VMEM((number,) + shape, BF16) for shape in of]
    one = lambda of: [pltpu.VMEM(shape, BF16) for shape in of]
    every = total + crossing
    scratch = slots(8, shapes) + slots(4, shapes) + slots(7, shapes[:total])
    scratch += slots(4, shapes[total:]) + one(shapes[total:]) + one(shapes[:total])
    scratch += one(shapes[count:total])
    scratch += [sem((7, total))] * 2 + [sem((7, count))] * 2 + [sem((8, count))] * 2 + [sem((count,))]
    scratch += [sem((8, crossing))] * 2 + [sem((len(pairs),))] * 2 + [sem((8, every))] * 3
    outs = pl.pallas_call(
        lambda *refs: ring_kernel(shapes[:total], crossing, pairs, *refs),
        out_shape=[jax.ShapeDtypeStruct(a.shape, BF16) for a in arrays[:count]],
        in_specs=[hbm] * every,
        out_specs=[hbm] * count,
        scratch_shapes=scratch,
        compiler_params=pltpu.CompilerParams(
            collective_id=1, has_side_effects=True, vmem_limit_bytes=RING_VMEM_LIMIT
        ),
        cost_estimate=pl.CostEstimate(
            flops=2 * sum(g.size for g in grads),
            bytes_accessed=6 * sum(g.size for g in grads),
            transcendentals=0,
        ),
    )(*arrays)
    return [o.reshape(g.shape) for o, g in zip(outs, grads)]


def unstack_qkv(total):
    depth = total.shape[0] // 3
    return jnp.stack([total[i * depth : (i + 1) * depth] for i in range(3)], axis=1)


def sum_small(links, values):
    if links.fast:
        values = values + links.over_x(values)
        for bit in (1, 2, 4, 8):
            values = values + links.over(bit, values)
        return values
    return lax.psum(values, ("dp", "freq"))


def own_images(links, values):
    count = values.shape[0] // links.shards
    return lax.dynamic_slice_in_dim(values, links.place * count, count, 0)


def reduce_rows(links, partial):
    if links.fast:
        keep, send = halves(partial, links.place, 0)
        return keep + links.over_x(send.astype(BF16)).astype(F32)
    return lax.psum_scatter(
        partial.astype(BF16), "freq", scatter_dimension=0, tiled=True
    ).astype(F32)


def gather_rows(links, values):
    if links.fast:
        return ordered(links.place, values, links.over_x(values), 0)
    return lax.all_gather(values, "freq", axis=0, tiled=True)


def block_forward(stream, gains, biases, attention, mlp, attend_all, head_size):
    normed = layer_norm(stream, gains[0], biases[0])
    middle = stream
    heads = []
    for weight_qkv, _ in attention:
        queries = (dot(normed, weight_qkv[0]) * head_size ** (-0.5)).astype(BF16)
        keys = dot(normed, weight_qkv[1]).astype(BF16)
        values = dot(normed, weight_qkv[2]).astype(BF16)
        heads.append((queries, keys, values))
    mixed = attend_all(heads)
    heads = [(*head, mix) for head, mix in zip(heads, mixed)]
    for (_, weight_out), mix in zip(attention, mixed):
        middle = middle + dot(mix, weight_out)
    normed_mid = layer_norm(middle, gains[1], biases[1])
    result = middle
    units = []
    for weight_up, weight_down in mlp():
        active, slope = up_projection(normed_mid, weight_up)
        result = result + dot(active, weight_down)
        units.append((active, slope))
    return result, (stream, normed, heads, middle, normed_mid, units)


def block_backward(
    grad, gains, attention, mlp, counts, seq, head_size, masked, saved
):
    stream, normed, heads, middle, normed_mid, units = saved
    low = grad.astype(BF16)
    down_grads, up_grads, grad_normed = [], [], 0.0
    for (weight_up, weight_down), (active, slope) in zip(mlp, units):
        grad_pre = (dot_nt(low, weight_down) * slope.astype(F32)).astype(BF16)
        grad_normed = grad_normed + dot_nt(grad_pre, weight_up)
        down_grads.append(dot_tn(active, low).astype(BF16))
        up_grads.append(dot_tn(normed_mid, grad_pre).astype(BF16))
    grad_in, mid_gain, mid_bias = layer_norm_back(grad_normed, middle, gains[1])
    grad = grad + grad_in
    low = grad.astype(BF16)
    out_grads, qkv_grads, grad_normed = [], [], 0.0
    for (weight_qkv, weight_out), (queries, keys, values, mixed) in zip(attention, heads):
        grad_mixed = dot_nt(low, weight_out).astype(BF16)
        grads = attend_back(queries, keys, values, grad_mixed, counts, seq, head_size, masked)
        for i in range(3):
            grad_normed = grad_normed + dot_nt(grads[i], weight_qkv[i])
        out_grads.append(dot_tn(mixed, low).astype(BF16))
        qkv_grads.append([dot_tn(normed, grads[i]).astype(BF16) for i in range(3)])
    grad_in, first_gain, first_bias = layer_norm_back(grad_normed, stream, gains[0])
    return (
        grad + grad_in,
        (first_gain, mid_gain),
        (first_bias, mid_bias),
        (qkv_grads, out_grads, up_grads, down_grads),
    )


def local(
    pixels,
    band_group,
    mask_order,
    visible_count,
    scale_id,
    patch_weight,
    enc_qkv,
    enc_out,
    enc_up,
    enc_down,
    enc_gains,
    enc_biases,
    dec_embed,
    mask_token,
    dec_qkv,
    dec_out,
    dec_up,
    dec_down,
    dec_gains,
    dec_biases,
    head_weight,
    recon_cotangent,
):
    links = Links()
    images, _, pixel_width = pixels.shape
    own = images // links.shards
    own_slots = own * VIS
    rgb_width = min(RGB_PIX, pixel_width)

    slot_ids = mask_order[:, :VIS]
    one_hot = slot_ids[:, :, None] == jnp.arange(NPATCH)[None, None, :]
    picked = jnp.einsum(
        "bsp,bpc->bsc", one_hot.astype(BF16), pixels, preferred_element_type=F32
    ).astype(BF16)
    multi = (band_group == 0)[:, None, None]
    zero = jnp.zeros((), BF16)
    rgb_valid = links.place * pixel_width + jnp.arange(rgb_width) < RGB_PIX
    picked_multi = jnp.where(multi, picked, zero).reshape(images * VIS, pixel_width)
    picked_rgb = jnp.where(~multi & rgb_valid, picked[:, :, :rgb_width], zero)
    picked_rgb = picked_rgb.reshape(images * VIS, rgb_width)
    patch_rgb = patch_weight[1, :rgb_width]
    partial = dot(picked_multi, patch_weight[0]) + dot(picked_rgb, patch_rgb)
    stacked = lambda weight: jnp.stack([weight[:, i] for i in range(3)])
    enc_attention = [(stacked(enc_qkv), enc_out)]
    enc_mlp = [(enc_up, enc_down)]
    dec_attention = [(stacked(dec_qkv), dec_out)]
    dec_mlp = [(dec_up, dec_down)]
    cotangent = recon_cotangent.reshape(images * NPATCH, -1)
    if links.fast:
        keep, send = halves(partial, links.place, 0)
        got, *others, grad_partial = head_start(
            send.astype(BF16), *enc_attention[0], cotangent, head_weight
        )
        embedded = keep + got.astype(F32)
        enc_attention.append(tuple(others))
        grad_final = None
        embedded, mask_order, scale_id = lax.optimization_barrier((embedded, mask_order, scale_id))
        slot_ids = mask_order[:, :VIS]
    else:
        embedded = reduce_rows(links, partial)
        grad_final = reduce_rows(links, dot_nt(cotangent, head_weight))
        enc_attention = [tuple(map(whole_weight, enc_attention[0], (2, 0)))]
        enc_mlp = [tuple(map(whole_weight, enc_mlp[0], (1, 0)))]
        dec_attention = [tuple(map(whole_weight, dec_attention[0], (2, 0)))]
        dec_mlp = [tuple(map(whole_weight, dec_mlp[0], (1, 0)))]

    my_slots = own_images(links, slot_ids)
    my_count = own_images(links, visible_count)
    ratios = jnp.exp2(own_images(links, scale_id).astype(F32) - 1.0)
    stream = embedded + slot_codes(my_slots, ratios, D).reshape(own_slots, D)

    def encoder_attention(heads):
        if not links.fast:
            return [attend(*head, my_count, VIS, HDIM, True) for head in heads]
        weights = (*enc_mlp[0], *dec_attention[0], *dec_mlp[0])
        nonlocal grad_final
        own_mix, other_mix, *others = attend_fetch(*heads, my_count, VIS, HDIM, weights)
        keep, send = halves(lax.optimization_barrier((grad_partial, own_mix))[0], links.place, 0)
        grad_final = keep.astype(F32) + links.over_x(send).astype(F32)
        enc_mlp.append(tuple(others[:2]))
        dec_attention.append(tuple(others[2:4]))
        dec_mlp.append(tuple(others[4:]))
        return own_mix, other_mix

    stream, enc_saved = block_forward(
        stream, enc_gains, enc_biases, enc_attention, lambda: enc_mlp, encoder_attention, HDIM
    )
    latent = layer_norm(stream, enc_gains[2], enc_biases[2])
    lifted = dot(latent, dec_embed)

    live = jnp.arange(VIS)[None, :] < my_count[:, None]
    select = (my_slots[:, :, None] == jnp.arange(NPATCH)[None, None, :]) & live[:, :, None]
    hidden = 1.0 - jnp.sum(select.astype(F32), axis=1)[:, :, None]
    decoded = (
        jnp.einsum(
            "bsp,bse->bpe",
            select.astype(F32),
            lifted.reshape(own, VIS, DDEC),
            precision=HIGHEST,
        )
        + hidden * mask_token
        + grid_codes(ratios, DDEC)
    ).reshape(own * NPATCH, DDEC)
    decoder_attention = lambda heads: [
        attend(*head, my_count, NPATCH, DHDIM, False) for head in heads
    ]
    decoded, dec_saved = block_forward(
        decoded, dec_gains, dec_biases, dec_attention, lambda: dec_mlp, decoder_attention, DHDIM
    )
    final_own = layer_norm(decoded, dec_gains[2], dec_biases[2])

    final_all = gather_rows(links, final_own)
    reconstructions = dot(final_all, head_weight).astype(BF16).reshape(images, NPATCH, -1)
    head_grad = dot_tn(final_all, cotangent).astype(BF16)

    grad_in, dec_gain_2, dec_bias_2 = layer_norm_back(grad_final, decoded, dec_gains[2])
    grad_decoded, dec_gain_01, dec_bias_01, dec_grads = block_backward(
        grad_in, dec_gains, dec_attention, dec_mlp, my_count, NPATCH, DHDIM, False, dec_saved
    )
    grad_grid = grad_decoded.reshape(own, NPATCH, DDEC)
    mask_grad = jnp.sum(hidden * grad_grid, axis=(0, 1))
    grad_lifted = (
        jnp.einsum(
            "bsp,bpe->bse",
            select.astype(BF16),
            grad_grid.astype(BF16),
            preferred_element_type=F32,
        )
        .astype(BF16)
        .reshape(own_slots, DDEC)
    )
    embed_grad = dot_tn(latent, grad_lifted).astype(BF16)
    grad_latent = dot_nt(grad_lifted, dec_embed)

    grad_in, enc_gain_2, enc_bias_2 = layer_norm_back(grad_latent, stream, enc_gains[2])
    grad_stream, enc_gain_01, enc_bias_01, enc_grads = block_backward(
        grad_in, enc_gains, enc_attention, enc_mlp, my_count, VIS, HDIM, True, enc_saved
    )

    grad_embedded = gather_rows(links, grad_stream.astype(BF16))
    patch_grads = [
        dot_tn(picked_multi, grad_embedded).astype(BF16),
        dot_tn(picked_rgb, grad_embedded).astype(BF16),
    ]
    multi_rows = jnp.repeat(band_group == 0, VIS)[:, None]
    back_multi = dot_nt(jnp.where(multi_rows, grad_embedded, zero), patch_weight[0])
    back_rgb = dot_nt(jnp.where(multi_rows, zero, grad_embedded), patch_rgb)
    back_rgb = jnp.where(rgb_valid, back_rgb, 0.0)
    back = back_multi + jnp.pad(back_rgb, ((0, 0), (0, pixel_width - rgb_width)))
    pixel_grad = jnp.einsum(
        "bsp,bsc->bpc",
        one_hot.astype(BF16),
        back.astype(BF16).reshape(images, VIS, pixel_width),
        preferred_element_type=F32,
    )

    dec_qkv_grads, dec_out_grads, dec_up_grads, dec_down_grads = dec_grads
    enc_qkv_grads, enc_out_grads, enc_up_grads, enc_down_grads = enc_grads
    stacked_qkv = lambda grads: [jnp.concatenate(g, 0) for g in grads]
    enc_stack = [
        (stacked_qkv(enc_qkv_grads), 1),
        (enc_out_grads, 0),
        (enc_up_grads, 1),
        (enc_down_grads, 0),
    ]
    dec_stack = [
        (stacked_qkv(dec_qkv_grads), 1),
        (dec_out_grads, 0),
        (dec_up_grads, 1),
        (dec_down_grads, 0),
    ]
    patch_grad = jnp.concatenate(patch_grads, 0)
    if links.fast:
        stacks = [grads for grads, _ in enc_stack[:3] + dec_stack]
        enc_last = enc_stack[3][0]
        late = [grads[0] for grads in stacks] + [embed_grad, enc_last[0], head_grad, patch_grad]
        late = ring_sums(
            late, [grads[1] for grads in stacks] + [embed_grad], {8: enc_last[1]}, {10}
        )
        late = [total.astype(F32) for total in late]
        enc_totals = [unstack_qkv(late[0]), late[1], late[2], late[8]]
        dec_totals = [unstack_qkv(late[3])] + late[4:7]
        embed_total, head_total = late[7], late[9]
        patch_total = jnp.pad(late[10], ((0, pixel_width - rgb_width), (0, 0)))
        patch_total = patch_total.reshape(2, pixel_width, D)
    else:
        reduced = []
        for stack in (dec_stack, enc_stack):
            parts = [
                lax.psum_scatter(g[0], "freq", scatter_dimension=axis, tiled=True)
                for g, axis in stack
            ]
            parts = [lax.psum(part, "dp").astype(F32) for part in parts]
            parts[0] = unstack_qkv(parts[0])
            reduced.append(parts)
        dec_totals, enc_totals = reduced
        embed_total = lax.psum(embed_grad, ("dp", "freq")).astype(F32)
        head_total = lax.psum(head_grad, "dp").astype(F32)
        patch_sum = lax.psum(patch_grad, "dp").astype(F32)
        patch_total = jnp.stack(
            [
                patch_sum[:pixel_width],
                jnp.pad(patch_sum[pixel_width:], ((0, pixel_width - rgb_width), (0, 0))),
            ]
        )
    small = [*enc_gain_01, enc_gain_2, *enc_bias_01, enc_bias_2]
    small += [*dec_gain_01, dec_gain_2, *dec_bias_01, dec_bias_2, mask_grad]
    small = sum_small(links, jnp.concatenate(small).reshape(-1, LANES)).reshape(-1)
    enc_end, dec_end = 6 * D, 6 * D + 6 * DDEC
    enc_small = small[:enc_end].reshape(2, 3, D)
    dec_small = small[enc_end:dec_end].reshape(2, 3, DDEC)
    return (
        reconstructions,
        pixel_grad,
        patch_total,
        *enc_totals,
        enc_small[0],
        enc_small[1],
        embed_total,
        small[dec_end:],
        *dec_totals,
        dec_small[0],
        dec_small[1],
        head_total,
    )


def solution(mesh):
    return jax.shard_map(
        local,
        mesh=mesh,
        in_specs=(
            P("dp", None, "freq"),
            P("dp"),
            P("dp", None),
            P("dp"),
            P("dp"),
            P(None, "freq", None),
            P(None, None, "freq"),
            P("freq", None),
            P(None, "freq"),
            P("freq", None),
            P(),
            P(),
            P(),
            P(),
            P(None, None, "freq"),
            P("freq", None),
            P(None, "freq"),
            P("freq", None),
            P(),
            P(),
            P(None, "freq"),
            P("dp", None, "freq"),
        ),
        out_specs=(
            P("dp", None, "freq"),
            P("dp", None, "freq"),
            P(None, "freq", None),
            P(None, None, "freq"),
            P("freq", None),
            P(None, "freq"),
            P("freq", None),
            P(),
            P(),
            P(),
            P(),
            P(None, None, "freq"),
            P("freq", None),
            P(None, "freq"),
            P("freq", None),
            P(),
            P(),
            P(None, "freq"),
        ),
        check_vma=False,
    )
```

```python
import math

import jax
import jax.numpy as jnp
from jax import lax
from jax.experimental import pallas as pl
from jax.experimental.pallas import tpu as pltpu
from jax.sharding import PartitionSpec as P

D = 1024
HDIM = 64
DDEC = 512
DHDIM = 32
RGB_PIX = 768
SIDE = 16
NPATCH = 256
VIS = 64

HIGHEST = lax.Precision.HIGHEST
EPSILON = 1e-06
MASKED = -1e30
BF16 = jnp.bfloat16
F32 = jnp.float32
LANES = 128
MIB = 1024 * 1024
RING_VMEM_LIMIT = 58 * MIB
MESH = pl.DeviceIdType.MESH


def dot(left, right):
    return jnp.dot(left, right, preferred_element_type=F32)


def dot_tn(left, right):
    return lax.dot_general(left, right, (((0,), (0,)), ((), ())), preferred_element_type=F32)


def dot_nt(left, right):
    return lax.dot_general(left, right, (((1,), (1,)), ((), ())), preferred_element_type=F32)


def normalize(values):
    center = values - jnp.mean(values, -1, keepdims=True)
    rstd = lax.rsqrt(jnp.mean(center * center, -1, keepdims=True) + EPSILON)
    return center * rstd, rstd


def layer_norm(values, scales, shifts):
    return (normalize(values)[0] * scales + shifts).astype(BF16)


def layer_norm_back(grad, values, scales):
    unit, rstd = normalize(values)
    scaled = grad * scales
    mean_grad = jnp.mean(scaled, -1, keepdims=True)
    mean_along = jnp.mean(scaled * unit, -1, keepdims=True)
    grad_in = rstd * (scaled - mean_grad - unit * mean_along)
    return grad_in, jnp.sum(grad * unit, 0), jnp.sum(grad, 0)


def code_tables(ratios, features):
    quarter = features // 4
    index_f = jnp.arange(quarter, dtype=F32)
    frequencies = jnp.exp(index_f * (-math.log(10000.0) / quarter))
    places = jnp.arange(SIDE).astype(F32)
    angle = (places[None, :] * ratios[:, None])[..., None] * frequencies
    return jnp.concatenate([jnp.sin(angle), jnp.cos(angle)], -1)


def slot_codes(slot_ids, ratios, features):
    table = code_tables(ratios, features)
    places = jnp.arange(SIDE)
    row = (slot_ids[..., None] // SIDE == places).astype(F32)
    col = (slot_ids[..., None] % SIDE == places).astype(F32)
    pick = lambda one_hot: jnp.einsum("bsp,bpf->bsf", one_hot, table, precision=HIGHEST)
    return jnp.concatenate([pick(row), pick(col)], -1)


def grid_codes(ratios, features):
    table = code_tables(ratios, features)
    images, _, half = table.shape
    row = jnp.broadcast_to(table[:, :, None, :], (images, SIDE, SIDE, half))
    col = jnp.broadcast_to(table[:, None, :, :], (images, SIDE, SIDE, half))
    return jnp.concatenate([row, col], -1).reshape(images, NPATCH, features)


def head_rows(values, head_size, heads):
    lane = lax.broadcasted_iota(jnp.int32, (1, LANES), 1)
    return jnp.concatenate(
        [jnp.where(lane // head_size == h, values, 0).astype(BF16) for h in heads], 0
    )


def head_parts(values, head_size, seq, merge):
    return [
        values[j * head_size : (j + 1) * head_size, j * seq : (j + 1) * seq] for j in range(merge)
    ]


def masked_scores(keys, queries, valid):
    scores = dot_nt(keys, queries)
    if valid is not None:
        scores = jnp.where(valid > 0.0, scores, MASKED)
    return scores


def attend_rows(head_size, merge, q_ref, k_ref, v_ref, o_ref, p_ref, valid):
    seq, width = q_ref.shape
    for g in range(width // LANES):
        lanes = slice(g * LANES, (g + 1) * LANES)
        queries, keys, values = q_ref[:, lanes], k_ref[:, lanes], v_ref[:, lanes]
        values_t = jnp.transpose(values)
        parts = []
        for h in range(0, LANES // head_size, merge):
            scores = masked_scores(
                keys, head_rows(queries, head_size, range(h, h + merge)), valid
            )
            top = jnp.max(scores, 0, keepdims=True)
            power = jnp.exp(scores - top)
            weights = (power * (1.0 / jnp.sum(power, 0, keepdims=True))).astype(BF16)
            p_ref[(g * LANES // head_size + h) // merge] = weights
            rows = slice(h * head_size, (h + merge) * head_size)
            parts += head_parts(dot(values_t[rows], weights), head_size, seq, merge)
        o_ref[:, lanes] = jnp.transpose(jnp.concatenate(parts, 0)).astype(BF16)


def attend_back_rows(
    head_size, merge, q_ref, k_ref, v_ref, p_ref, g_ref, dq_ref, dk_ref, dv_ref
):
    seq, width = q_ref.shape
    factor = head_size ** (-0.5)
    for g in range(width // LANES):
        lanes = slice(g * LANES, (g + 1) * LANES)
        queries, keys, values, grads = (
            q_ref[:, lanes],
            k_ref[:, lanes],
            v_ref[:, lanes],
            g_ref[:, lanes],
        )
        keys_t = jnp.transpose(keys)
        parts, dk_sum, dv_sum = [], 0.0, 0.0
        for h in range(0, LANES // head_size, merge):
            own_q = head_rows(queries, head_size, range(h, h + merge))
            own_g = head_rows(grads, head_size, range(h, h + merge))
            weights = p_ref[(g * LANES // head_size + h) // merge]
            dv_sum += dot(weights, own_g)
            grad_weights = dot_nt(values, own_g)
            product = weights.astype(F32) * grad_weights
            along = jnp.sum(product, 0, keepdims=True)
            grad_scores = (product - weights.astype(F32) * along).astype(BF16)
            dk_sum += dot(grad_scores, own_q)
            rows = slice(h * head_size, (h + merge) * head_size)
            grad_q = dot(keys_t[rows], grad_scores) * factor
            parts += head_parts(grad_q, head_size, seq, merge)
        dq_ref[:, lanes] = jnp.transpose(jnp.concatenate(parts, 0)).astype(BF16)
        dk_ref[:, lanes] = dk_sum.astype(BF16)
        dv_ref[:, lanes] = dv_sum.astype(BF16)


def valid_rows(counts, seq, merge):
    valid = (jnp.arange(seq)[None, :, None] < counts[:, None, None]).astype(F32)
    return jnp.broadcast_to(valid, (counts.shape[0], seq, merge * seq))


def row_block(seq, width):
    return pl.BlockSpec((seq, width), lambda i: (i, 0))


def weight_block(seq, width, head_size):
    merge = LANES // head_size
    return pl.BlockSpec((None, width // LANES, seq, merge * seq), lambda i: (i, 0, 0, 0))


def weight_shape(images, seq, width, head_size):
    merge = LANES // head_size
    return jax.ShapeDtypeStruct((images, width // LANES, seq, merge * seq), BF16)


def attention_cost(rows, seq, width, head_size, shards, products, arrays):
    merge = LANES // head_size
    return pl.CostEstimate(
        flops=2 * shards * products * rows * seq * width * merge,
        bytes_accessed=2 * shards * rows * (arrays * width + seq * width // head_size),
        transcendentals=shards * rows * seq * width // head_size,
    )


def attend(queries, keys, values, counts, seq, head_size, masked):
    rows, width = queries.shape
    images, merge = rows // seq, LANES // head_size
    valid = [valid_rows(counts, seq, merge)] if masked else []

    def kernel(*refs):
        mask = refs[3][...] if masked else None
        attend_rows(head_size, merge, *refs[:3], *refs[3 + len(valid) :], mask)

    return pl.pallas_call(
        kernel,
        grid=(images,),
        in_specs=[row_block(seq, width)] * 3
        + [pl.BlockSpec((None,) + v.shape[1:], lambda i: (i, 0, 0)) for v in valid],
        out_specs=[row_block(seq, width), weight_block(seq, width, head_size)],
        out_shape=[
            jax.ShapeDtypeStruct((rows, width), BF16),
            weight_shape(images, seq, width, head_size),
        ],
        compiler_params=pltpu.CompilerParams(vmem_limit_bytes=20 * MIB),
        cost_estimate=attention_cost(rows, seq, width, head_size, 1, 2, 4),
    )(queries, keys, values, *valid)


def attend_back(queries, keys, values, weights, grads, seq, head_size):
    rows, width = queries.shape
    images, merge = rows // seq, LANES // head_size
    return pl.pallas_call(
        lambda *refs: attend_back_rows(head_size, merge, *refs),
        grid=(images,),
        in_specs=[row_block(seq, width)] * 3
        + [weight_block(seq, width, head_size), row_block(seq, width)],
        out_specs=[row_block(seq, width)] * 3,
        out_shape=[jax.ShapeDtypeStruct((rows, width), BF16)] * 3,
        compiler_params=pltpu.CompilerParams(vmem_limit_bytes=20 * MIB),
        cost_estimate=attention_cost(rows, seq, width, head_size, 1, 4, 7),
    )(queries, keys, values, weights, grads)


def up_kernel(x_ref, w_ref, active_ref, slope_ref):
    pre = dot(x_ref[...], w_ref[...])
    cdf = 0.5 + 0.5 * lax.erf(pre * math.sqrt(0.5))
    density = jnp.exp(-0.5 * pre * pre) * (1.0 / math.sqrt(2.0 * math.pi))
    active_ref[...] = (pre * cdf).astype(BF16)
    slope_ref[...] = (cdf + pre * density).astype(BF16)


def up_projection(rows_in, weight):
    rows, depth = rows_in.shape
    width = weight.shape[1]
    row_block = math.gcd(rows, 512)
    col_block = math.gcd(width, 512)
    out = jax.ShapeDtypeStruct((rows, width), BF16)
    spec = pl.BlockSpec((row_block, col_block), lambda i, j: (i, j))
    return pl.pallas_call(
        up_kernel,
        grid=(rows // row_block, width // col_block),
        in_specs=[
            pl.BlockSpec((row_block, depth), lambda i, j: (i, 0)),
            pl.BlockSpec((depth, col_block), lambda i, j: (0, j)),
        ],
        out_specs=[spec, spec],
        out_shape=[out, out],
        compiler_params=pltpu.CompilerParams(vmem_limit_bytes=20 * MIB),
        cost_estimate=pl.CostEstimate(
            flops=2 * rows * depth * width,
            bytes_accessed=2 * (rows * depth + depth * width + 2 * rows * width),
            transcendentals=2 * rows * width,
        ),
    )(rows_in, weight)


def product_kernel(left_ref, right_ref, out_ref):
    out_ref[...] = dot(left_ref[...], right_ref[...]).astype(BF16)


def row_product(left, right):
    rows, depth = left.shape
    width = right.shape[1]
    block = math.gcd(rows, 512)
    return pl.pallas_call(
        product_kernel,
        grid=(rows // block,),
        in_specs=[
            pl.BlockSpec((block, depth), lambda i: (i, 0)),
            pl.BlockSpec((depth, width), lambda i: (0, 0)),
        ],
        out_specs=pl.BlockSpec((block, width), lambda i: (i, 0)),
        out_shape=jax.ShapeDtypeStruct((rows, width), BF16),
        compiler_params=pltpu.CompilerParams(vmem_limit_bytes=32 * MIB),
        cost_estimate=pl.CostEstimate(
            flops=2 * rows * depth * width,
            bytes_accessed=2 * (rows * depth + depth * width + rows * width),
            transcendentals=0,
        ),
    )(left, right)


class Links:
    def __init__(self):
        self.shards = lax.axis_size("freq")
        self.fast = self.shards == 2 and lax.axis_size("dp") == 16
        self.place = lax.axis_index("freq")
        index = lax.axis_index("dp")
        self.core = index % 2
        self.row = (index // 2) % 2
        depth = index // 4
        along = jnp.where(self.row == 0, depth, 7 - depth)
        self.rank = jnp.where(self.core == 0, along, (8 - along) % 8)
        cycle = [z * 4 for z in range(4)] + [z * 4 + 2 for z in range(3, -1, -1)]
        self.ring = []
        for i in range(8):
            self.ring.append((cycle[i], cycle[(i + 1) % 8]))
            self.ring.append((cycle[i] + 1, cycle[(i + 7) % 8] + 1))

    def over_x(self, values):
        return lax.ppermute(values, "freq", [(0, 1), (1, 0)])

    def over(self, bit, values):
        return lax.ppermute(values, "dp", [(i, i ^ bit) for i in range(16)])

    def over_core(self, values):
        return self.over(1, values)

    def over_ring(self, values):
        return lax.ppermute(values, "dp", self.ring)


def halves(values, which, axis):
    size = values.shape[axis] // 2
    return (
        lax.dynamic_slice_in_dim(values, which * size, size, axis),
        lax.dynamic_slice_in_dim(values, (1 - which) * size, size, axis),
    )


def ordered(which, own, other, axis):
    return jnp.where(
        which == 0,
        jnp.concatenate([own, other], axis),
        jnp.concatenate([other, own], axis),
    )


class Fetch:
    STEPS = 4

    def __init__(self, sources, targets, items, send, recv):
        self.sources, self.targets, self.send, self.recv = sources, targets, send, recv
        self.items = items
        index, across = lax.axis_index("dp"), lax.axis_index("freq")
        core, row = index % 2, (index // 2) % 2
        self.quarter = index % 4
        self.next_quarter = self.quarter + 2 - 4 * row
        self.facing = (index, 1 - across)
        self.beside = (index + 2 - 4 * row, across)
        self.twin = (index + 1 - 2 * core, across)

    def greet(self):
        barrier = pltpu.get_barrier_semaphore()
        for partner in (self.facing, self.beside, self.twin):
            pl.semaphore_signal(barrier, inc=1, device_id=partner, device_id_type=MESH)
        pl.semaphore_wait(barrier, 3)

    def view(self, ref, quarter, part, parts):
        rows = ref.shape[-2] // (4 * parts)
        place = pl.ds(pl.multiple_of((quarter * parts + part) * rows, 16), rows)
        return ref.at[:, place] if len(ref.shape) == 3 else ref.at[place]

    def copy(self, i, step):
        quarter = self.next_quarter if step == 3 else self.quarter
        array, part, parts = self.items[i]
        target = self.view(self.targets[array], quarter, part, parts)
        source = self.view(self.sources[array], quarter, part, parts)
        return pltpu.make_async_remote_copy(
            src_ref=source if step == 0 else target,
            dst_ref=target,
            send_sem=self.send.at[step, i],
            recv_sem=self.recv.at[step, i],
            device_id=(self.facing, self.beside, self.twin, self.twin)[step],
            device_id_type=MESH,
        )

    def start(self, items):
        for i in items:
            self.copy(i, 0).start()

    def pass_on(self, items):
        for i in items:
            self.copy(i, 0).wait_recv()
            self.copy(i, 1).start()
            self.copy(i, 2).start()

    def pass_on_last(self, items):
        for i in items:
            self.copy(i, 1).wait_recv()
            self.copy(i, 3).start()

    def finish(self):
        for i in range(len(self.items)):
            for step in range(self.STEPS):
                self.copy(i, step).wait_send()
                if step >= 2:
                    self.copy(i, step).wait_recv()


def head_start_kernel(rows_ref, qkv_ref, out_ref, cot_ref, head_ref, *refs):
    got_ref, new_qkv, new_out, partial_ref, tiles, sums = refs[:6]
    send, recv, row_send, row_recv, tile_sem, sum_sem = refs[6:]
    items = [(0, 0, 1), (1, 0, 1)]
    fetch = Fetch([qkv_ref, out_ref], [new_qkv, new_out], items, send, recv)
    fetch.greet()
    rows_copy = pltpu.make_async_remote_copy(
        src_ref=rows_ref,
        dst_ref=got_ref,
        send_sem=row_send,
        recv_sem=row_recv,
        device_id=fetch.facing,
        device_id_type=MESH,
    )
    fetch.start([0, 1])
    tile = tiles.shape[1]
    count = cot_ref.shape[0] // tile

    def load(i, slot):
        return pltpu.make_async_copy(
            cot_ref.at[pl.ds(i * tile, tile)], tiles.at[slot], tile_sem.at[slot]
        )

    def store(i, slot):
        return pltpu.make_async_copy(
            sums.at[slot], partial_ref.at[pl.ds(i * tile, tile)], sum_sem.at[slot]
        )

    load(0, 0).start()
    load(1, 1).start()

    def body(pair, carry):
        for slot in range(2):
            i = pair * 2 + slot
            load(i, slot).wait()

            @pl.when(pair > 0)
            def _():
                store(i - 2, slot).wait()

            sums[slot] = dot_nt(tiles[slot], head_ref[...]).astype(BF16)
            store(i, slot).start()

            @pl.when(pair < count // 2 - 1)
            def _():
                load(i + 2, slot).start()

        return carry

    lax.fori_loop(0, count // 2, body, 0)
    for slot in range(2):
        store(count - 2 + slot, slot).wait()
    fetch.pass_on([0, 1])
    rows_copy.start()
    fetch.pass_on_last([0, 1])
    fetch.finish()
    rows_copy.wait()


def head_start(rows, weight_qkv, weight_out, cotangent, head_weight):
    hbm, vmem = pl.BlockSpec(memory_space=pl.ANY), pl.BlockSpec(memory_space=pltpu.VMEM)
    sem, shape = pltpu.SemaphoreType.DMA, lambda a: jax.ShapeDtypeStruct(a.shape, a.dtype)
    count, columns = cotangent.shape
    width = head_weight.shape[0]
    tile = 256
    return pl.pallas_call(
        head_start_kernel,
        out_shape=[
            shape(rows),
            shape(weight_qkv),
            shape(weight_out),
            jax.ShapeDtypeStruct((count, width), BF16),
        ],
        in_specs=[hbm] * 4 + [vmem],
        out_specs=[hbm] * 4,
        scratch_shapes=[
            pltpu.VMEM((2, tile, columns), BF16),
            pltpu.VMEM((2, tile, width), BF16),
            sem((4, 2)),
            sem((4, 2)),
            sem,
            sem,
            sem((2,)),
            sem((2,)),
        ],
        compiler_params=pltpu.CompilerParams(
            collective_id=2, has_side_effects=True, vmem_limit_bytes=20 * MIB
        ),
        cost_estimate=pl.CostEstimate(
            flops=2 * count * columns * width,
            bytes_accessed=2 * count * columns,
            transcendentals=0,
        ),
    )(rows, weight_qkv, weight_out, cotangent, head_weight)


ATTEND_ITEMS = [(i, part, 2) for i in range(2) for part in range(2)]
ATTEND_ITEMS += [(i, 0, 1) for i in range(2, 6)]


def attend_fetch_kernel(head_size, merge, steps, *refs):
    own, other, valid_ref, sources = refs[:3], refs[3:6], refs[6], refs[7:13]
    own_out, other_out, targets = refs[13:15], refs[15:17], refs[17:23]
    send, recv = refs[23:]
    fetch = Fetch(sources, targets, ATTEND_ITEMS, send, recv)
    count, step = len(ATTEND_ITEMS), pl.program_id(0)

    @pl.when(step == 0)
    def _():
        fetch.greet()
        fetch.start([0])

    pl.when(step == steps // 2)(lambda: fetch.start([1]))

    @pl.when(step == steps - 2)
    def _():
        fetch.pass_on([0])
        fetch.start([2])

    valid = valid_ref[...]
    attend_rows(head_size, merge, *own, *own_out, valid)
    attend_rows(head_size, merge, *other, *other_out, valid)

    @pl.when(step == steps - 1)
    def _():
        for i in range(1, count):
            fetch.pass_on([i])
            fetch.start([i + 2] if i + 2 < count else [])
            fetch.pass_on_last([i - 1])
        fetch.pass_on_last([count - 1])
        fetch.finish()


def attend_fetch(own, other, counts, seq, head_size, weights):
    rows, width = own[0].shape
    images, merge = rows // seq, LANES // head_size
    block = row_block(seq, width)
    hbm, sem = pl.BlockSpec(memory_space=pl.ANY), pltpu.SemaphoreType.DMA
    valid = valid_rows(counts, seq, merge)
    out = [
        jax.ShapeDtypeStruct((rows, width), BF16),
        weight_shape(images, seq, width, head_size),
    ]
    return pl.pallas_call(
        lambda *refs: attend_fetch_kernel(head_size, merge, images, *refs),
        grid=(images,),
        out_shape=out * 2 + [jax.ShapeDtypeStruct(w.shape, w.dtype) for w in weights],
        in_specs=[block] * 6
        + [pl.BlockSpec((None,) + valid.shape[1:], lambda i: (i, 0, 0))]
        + [hbm] * len(weights),
        out_specs=[block, weight_block(seq, width, head_size)] * 2 + [hbm] * len(weights),
        scratch_shapes=[sem((4, len(ATTEND_ITEMS)))] * 2,
        compiler_params=pltpu.CompilerParams(
            collective_id=3, has_side_effects=True, vmem_limit_bytes=20 * MIB
        ),
        cost_estimate=attention_cost(rows, seq, width, head_size, 2, 2, 4),
    )(*own, *other, valid, *weights)


def attend_back_swap_kernel(head_size, merge, steps, *refs):
    own, other, rows_ref = refs[:5], refs[5:10], refs[10]
    own_out, other_out, got_ref = refs[11:14], refs[14:17], refs[17]
    send, recv = refs[18:]
    facing = (lax.axis_index("dp"), 1 - lax.axis_index("freq"))
    swap = pltpu.make_async_remote_copy(
        src_ref=rows_ref,
        dst_ref=got_ref,
        send_sem=send,
        recv_sem=recv,
        device_id=facing,
        device_id_type=MESH,
    )

    @pl.when(pl.program_id(0) == 0)
    def _():
        barrier = pltpu.get_barrier_semaphore()
        pl.semaphore_signal(barrier, inc=1, device_id=facing, device_id_type=MESH)
        pl.semaphore_wait(barrier, 1)
        swap.start()

    attend_back_rows(head_size, merge, *own, *own_out)
    attend_back_rows(head_size, merge, *other, *other_out)

    @pl.when(pl.program_id(0) == steps - 1)
    def _():
        swap.wait()


def attend_back_swap(own, other, seq, head_size, rows_out):
    rows, width = own[0].shape
    images, merge = rows // seq, LANES // head_size
    block = row_block(seq, width)
    hbm = pl.BlockSpec(memory_space=pl.ANY)
    out = jax.ShapeDtypeStruct((rows, width), BF16)
    return pl.pallas_call(
        lambda *refs: attend_back_swap_kernel(head_size, merge, images, *refs),
        grid=(images,),
        out_shape=[out] * 6 + [jax.ShapeDtypeStruct(rows_out.shape, rows_out.dtype)],
        in_specs=([block] * 3 + [weight_block(seq, width, head_size), block]) * 2 + [hbm],
        out_specs=[block] * 6 + [hbm],
        scratch_shapes=[pltpu.SemaphoreType.DMA] * 2,
        compiler_params=pltpu.CompilerParams(
            collective_id=4, has_side_effects=True, vmem_limit_bytes=28 * MIB
        ),
        cost_estimate=attention_cost(rows, seq, width, head_size, 2, 4, 7),
    )(*own, *other, rows_out)


def whole_weight(weight, axis):
    return lax.all_gather(weight, "freq", axis=axis, tiled=True)


def core_sum(links, values, axis):
    keep, send = halves(values, links.core, axis)
    return keep + links.over_core(send)


def ring_kernel(shapes, crossing, pairs, *refs):
    count = len(shapes) - len(pairs)
    total = len(shapes)
    every = total + crossing

    def take(number):
        nonlocal refs
        head, refs = refs[:number], refs[number:]
        return head

    arrays, sums = take(every), take(count)
    mine, twins = take(every), take(every)
    held, crossed, first, done = take(total), take(crossing), take(crossing), take(total)
    arrived = take(len(pairs))
    out_send, out_recv, back_send, back_recv, side_send, side_recv, own_sem = take(7)
    x_send, x_recv, end_send, end_recv, load_sem, core_send, core_recv = take(7)
    index, across = lax.axis_index("dp"), lax.axis_index("freq")
    core, row, depth = index % 2, (index // 2) % 2, index // 4
    along = depth * (1 - row) + (7 - depth) * row
    rank = (along * (1 - core) + (8 - along) * core) % 8
    twin_rank = (8 - rank) % 8

    def device(spot):
        spot = spot % 8
        side = spot // 4
        return (spot * (1 - side) + (7 - spot) * side) * 4 + side * 2 + core

    way = 1 - 2 * core
    after, before = (device(along + way + 8), across), (device(along - way + 8), across)
    twin, facing = (index + 1 - 2 * core, across), (index, 1 - across)
    barrier = pltpu.get_barrier_semaphore()
    for partner in (after, before, twin, facing):
        pl.semaphore_signal(barrier, inc=1, device_id=partner, device_id_type=MESH)
    pl.semaphore_wait(barrier, 4)

    def copy(src, dst, send, recv, partner):
        return pltpu.make_async_remote_copy(
            src_ref=src,
            dst_ref=dst,
            send_sem=send,
            recv_sem=recv,
            device_id=partner,
            device_id_type=MESH,
        )

    def chunk(ref, half, place):
        if ref.shape[0] == 16:
            return ref.at[half * 8 + place]
        width = ref.shape[2] // 2
        return ref.at[place, :, pl.ds(pl.multiple_of(half * width, 128), width)]

    def load(i, step):
        place = (rank + 8 - step) % 8
        return pltpu.make_async_copy(
            chunk(arrays[i], core, place), mine[i].at[step], load_sem.at[step, i]
        )

    def coreward(i, step):
        place = (twin_rank + 8 - step) % 8
        return copy(
            chunk(arrays[i], 1 - core, place),
            twins[i].at[step % 4],
            core_send.at[step, i],
            core_recv.at[step, i],
            twin,
        )

    def core_sum(i, step, more):
        load(i, step).wait()
        coreward(i, step).wait_recv()
        value = mine[i][step] + twins[i][step % 4]
        mine[i][step] = value
        if more:
            coreward(i, step + 2).start()
        return value

    def facingward(i, step):
        return copy(
            mine[total + i].at[step],
            crossed[i].at[step % 4],
            x_send.at[step, i],
            x_recv.at[step, i],
            facing,
        )

    def cross(i, step, more):
        core_sum(total + i, step, more)
        facingward(i, step).start()

    def own(i, step, more, later):
        value = core_sum(i, step, more)
        if i >= crossing:
            return value
        facingward(i, step).wait_recv()
        value = value + crossed[i][step % 4]
        if more:
            mine[i][step] = value
            cross(i, step + 2, later)
        return value

    def outward(i, step, src):
        return copy(src, held[i].at[step], out_send.at[step, i], out_recv.at[step, i], after)

    def backward(i, step, place, src):
        return copy(
            src,
            chunk(sums[i], core, place),
            back_send.at[step, i],
            back_recv.at[step, i],
            after,
        )

    def sideward(i, step, place, src):
        return copy(
            src, chunk(sums[i], core, place), side_send.at[step, i], side_recv.at[step, i], twin
        )

    def keep(i, place):
        return pltpu.make_async_copy(done[i], chunk(sums[i], core, place), own_sem.at[i])

    def lastward(j):
        return copy(done[count + j], arrived[j], end_send.at[j], end_recv.at[j], facing)

    order = list(range(crossing, total)) + list(range(crossing))
    crossers = list(range(total, every))
    for step in range(8):
        for i in crossers + order:
            load(i, step).start()
            if step < 2:
                coreward(i, step).start()
    for step in range(2):
        for i in range(crossing):
            cross(i, step, True)
    for i in order:
        first_ref = mine[i].at[0] if i >= crossing else first[i]
        value = own(i, 0, True, True)
        if i < crossing:
            first[i][...] = value
        outward(i, 0, first_ref).start()

    def out_step(more, later):
        def body(step, carry):
            for i in order:
                outward(i, step, held[i].at[step]).wait_recv()
                held[i][step] = held[i][step] + own(i, step + 1, more, later)
                outward(i, step + 1, held[i].at[step]).start()
            return carry

        return body

    lax.fori_loop(0, 3, out_step(True, True), 0)
    lax.fori_loop(3, 5, out_step(True, False), 0)
    lax.fori_loop(5, 6, out_step(False, False), 0)
    place = (rank + 1) % 8
    for i in range(count, total):
        outward(i, 6, held[i].at[6]).wait_recv()
        done[i][...] = held[i][6] + own(i, 7, False, False)
        lastward(i - count).start()
    for i in order:
        if i >= count:
            continue
        outward(i, 6, held[i].at[6]).wait_recv()
        value = held[i][6] + own(i, 7, False, False)
        if i in pairs:
            lastward(pairs.index(i)).wait_recv()
            value = value + arrived[pairs.index(i)][...]
        done[i][...] = value
        backward(i, 0, place, done[i]).start()
        sideward(i, 0, place, done[i]).start()
        keep(i, place).start()

    def back_step(step, carry):
        place = (rank + 8 - step) % 8
        for i in range(count):
            ref = chunk(sums[i], core, place)
            backward(i, step, place, ref).wait_recv()
            backward(i, step + 1, place, ref).start()
            sideward(i, step + 1, place, ref).start()
        return carry

    lax.fori_loop(0, 6, back_step, 0)
    place = (rank + 2) % 8
    for i in range(count):
        ref = chunk(sums[i], core, place)
        backward(i, 6, place, ref).wait_recv()
        sideward(i, 7, place, ref).start()

    def end_step(step, carry):
        for i in range(total):
            outward(i, step, held[i].at[step]).wait_send()
        for i in range(count):
            backward(i, step, step, chunk(sums[i], core, step)).wait_send()
            sideward(i, step, step, chunk(sums[i], core, step)).wait_send()
            sideward(i, step, step, chunk(sums[i], core, step)).wait_recv()
        for i in range(crossing):
            facingward(i, step).wait_send()
        for i in range(every):
            coreward(i, step).wait_send()
        return carry

    lax.fori_loop(0, 7, end_step, 0)
    for i in range(count):
        sideward(i, 7, 7, chunk(sums[i], core, 7)).wait_send()
        sideward(i, 7, 7, chunk(sums[i], core, 7)).wait_recv()
        keep(i, 7).wait()
    for i in range(crossing):
        facingward(i, 7).wait_send()
    for i in range(every):
        coreward(i, 7).wait_send()
    for j in range(len(pairs)):
        lastward(j).wait_send()


def ring_sums(grads, cross, extra, columns):
    count, crossing, pairs = len(grads), len(cross), sorted(extra)
    total = count + len(pairs)
    arrays = []
    for i, grad in enumerate(list(grads) + [extra[i] for i in pairs] + list(cross)):
        pieces = 8 if i in columns else 16
        arrays.append(grad.reshape(pieces, grad.shape[0] // pieces, grad.shape[1]))
    shapes = [
        (a.shape[1], a.shape[2] // 2 if i in columns else a.shape[2])
        for i, a in enumerate(arrays)
    ]
    hbm, sem = pl.BlockSpec(memory_space=pl.ANY), pltpu.SemaphoreType.DMA
    slots = lambda number, of: [pltpu.VMEM((number,) + shape, BF16) for shape in of]
    one = lambda of: [pltpu.VMEM(shape, BF16) for shape in of]
    every = total + crossing
    scratch = slots(8, shapes) + slots(4, shapes) + slots(7, shapes[:total])
    scratch += slots(4, shapes[total:]) + one(shapes[total:]) + one(shapes[:total])
    scratch += one(shapes[count:total])
    scratch += [sem((7, total))] * 2 + [sem((7, count))] * 2 + [sem((8, count))] * 2 + [sem((count,))]
    scratch += [sem((8, crossing))] * 2 + [sem((len(pairs),))] * 2 + [sem((8, every))] * 3
    outs = pl.pallas_call(
        lambda *refs: ring_kernel(shapes[:total], crossing, pairs, *refs),
        out_shape=[jax.ShapeDtypeStruct(a.shape, BF16) for a in arrays[:count]],
        in_specs=[hbm] * every,
        out_specs=[hbm] * count,
        scratch_shapes=scratch,
        compiler_params=pltpu.CompilerParams(
            collective_id=1, has_side_effects=True, vmem_limit_bytes=RING_VMEM_LIMIT
        ),
        cost_estimate=pl.CostEstimate(
            flops=2 * sum(g.size for g in grads),
            bytes_accessed=6 * sum(g.size for g in grads),
            transcendentals=0,
        ),
    )(*arrays)
    return [o.reshape(g.shape) for o, g in zip(outs, grads)]


def unstack_qkv(total):
    depth = total.shape[0] // 3
    return jnp.stack([total[i * depth : (i + 1) * depth] for i in range(3)], axis=1)


def own_images(links, values):
    count = values.shape[0] // links.shards
    return lax.dynamic_slice_in_dim(values, links.place * count, count, 0)


def reduce_rows(links, partial):
    if links.fast:
        keep, send = halves(partial, links.place, 0)
        return keep + links.over_x(send.astype(BF16)).astype(F32)
    return lax.psum_scatter(
        partial.astype(BF16), "freq", scatter_dimension=0, tiled=True
    ).astype(F32)


def gather_rows(links, values):
    if links.fast:
        return ordered(links.place, values, links.over_x(values), 0)
    return lax.all_gather(values, "freq", axis=0, tiled=True)


def block_forward(stream, gains, biases, attention, mlp, attend_all, head_size):
    normed = layer_norm(stream, gains[0], biases[0])
    middle = stream
    heads = []
    for weight_qkv, _ in attention:
        queries = (dot(normed, weight_qkv[0]) * head_size ** (-0.5)).astype(BF16)
        keys = dot(normed, weight_qkv[1]).astype(BF16)
        values = dot(normed, weight_qkv[2]).astype(BF16)
        heads.append((queries, keys, values))
    mixed = attend_all(heads)
    heads = [(*head, weights, mix) for head, (mix, weights) in zip(heads, mixed)]
    for (_, weight_out), (mix, _) in zip(attention, mixed):
        middle = middle + dot(mix, weight_out)
    normed_mid = layer_norm(middle, gains[1], biases[1])
    result = middle
    units = []
    for weight_up, weight_down in mlp():
        active, slope = up_projection(normed_mid, weight_up)
        result = result + dot(active, weight_down)
        units.append((active, slope))
    return result, (stream, normed, heads, middle, normed_mid, units)


def block_backward(grad, gains, attention, mlp, attend_back_all, saved):
    stream, normed, heads, middle, normed_mid, units = saved
    low = grad.astype(BF16)
    down_grads, up_grads, grad_normed = [], [], 0.0
    for (weight_up, weight_down), (active, slope) in zip(mlp, units):
        grad_pre = (dot_nt(low, weight_down) * slope.astype(F32)).astype(BF16)
        grad_normed = grad_normed + dot_nt(grad_pre, weight_up)
        down_grads.append(dot_tn(active, low).astype(BF16))
        up_grads.append(dot_tn(normed_mid, grad_pre).astype(BF16))
    grad_in, mid_gain, mid_bias = layer_norm_back(grad_normed, middle, gains[1])
    grad = grad + grad_in
    low = grad.astype(BF16)
    out_grads, qkv_grads, grad_normed = [], [], 0.0
    grad_heads = [
        (*head[:4], dot_nt(low, weight_out).astype(BF16))
        for (_, weight_out), head in zip(attention, heads)
    ]
    for (weight_qkv, _), head, grads in zip(attention, heads, attend_back_all(grad_heads)):
        for i in range(3):
            grad_normed = grad_normed + dot_nt(grads[i], weight_qkv[i])
        out_grads.append(dot_tn(head[4], low).astype(BF16))
        qkv_grads.append([dot_tn(normed, grads[i]).astype(BF16) for i in range(3)])
    grad_in, first_gain, first_bias = layer_norm_back(grad_normed, stream, gains[0])
    return (
        grad + grad_in,
        (first_gain, mid_gain),
        (first_bias, mid_bias),
        (qkv_grads, out_grads, up_grads, down_grads),
    )


def local(
    pixels,
    band_group,
    mask_order,
    visible_count,
    scale_id,
    patch_weight,
    enc_qkv,
    enc_out,
    enc_up,
    enc_down,
    enc_gains,
    enc_biases,
    dec_embed,
    mask_token,
    dec_qkv,
    dec_out,
    dec_up,
    dec_down,
    dec_gains,
    dec_biases,
    head_weight,
    recon_cotangent,
):
    links = Links()
    images, _, pixel_width = pixels.shape
    own = images // links.shards
    own_slots = own * VIS
    rgb_width = min(RGB_PIX, pixel_width)

    slot_ids = mask_order[:, :VIS]
    one_hot = slot_ids[:, :, None] == jnp.arange(NPATCH)[None, None, :]
    picked = jnp.einsum(
        "bsp,bpc->bsc", one_hot.astype(BF16), pixels, preferred_element_type=F32
    ).astype(BF16)
    multi = (band_group == 0)[:, None, None]
    zero = jnp.zeros((), BF16)
    rgb_valid = links.place * pixel_width + jnp.arange(rgb_width) < RGB_PIX
    picked_multi = jnp.where(multi, picked, zero).reshape(images * VIS, pixel_width)
    picked_rgb = jnp.where(~multi & rgb_valid, picked[:, :, :rgb_width], zero)
    picked_rgb = picked_rgb.reshape(images * VIS, rgb_width)
    patch_rgb = patch_weight[1, :rgb_width]
    partial = dot(picked_multi, patch_weight[0]) + dot(picked_rgb, patch_rgb)
    stacked = lambda weight: jnp.stack([weight[:, i] for i in range(3)])
    enc_attention = [(stacked(enc_qkv), enc_out)]
    enc_mlp = [(enc_up, enc_down)]
    dec_attention = [(stacked(dec_qkv), dec_out)]
    dec_mlp = [(dec_up, dec_down)]
    cotangent = recon_cotangent.reshape(images * NPATCH, -1)
    if links.fast:
        keep, send = halves(partial, links.place, 0)
        got, *others, grad_partial = head_start(
            send.astype(BF16), *enc_attention[0], cotangent, head_weight
        )
        embedded = keep + got.astype(F32)
        enc_attention.append(tuple(others))
        grad_final = None
        embedded, mask_order, scale_id = lax.optimization_barrier((embedded, mask_order, scale_id))
        slot_ids = mask_order[:, :VIS]
    else:
        embedded = reduce_rows(links, partial)
        grad_final = reduce_rows(links, dot_nt(cotangent, head_weight))
        enc_attention = [tuple(map(whole_weight, enc_attention[0], (2, 0)))]
        enc_mlp = [tuple(map(whole_weight, enc_mlp[0], (1, 0)))]
        dec_attention = [tuple(map(whole_weight, dec_attention[0], (2, 0)))]
        dec_mlp = [tuple(map(whole_weight, dec_mlp[0], (1, 0)))]

    my_slots = own_images(links, slot_ids)
    my_count = own_images(links, visible_count)
    ratios = jnp.exp2(own_images(links, scale_id).astype(F32) - 1.0)
    stream = embedded + slot_codes(my_slots, ratios, D).reshape(own_slots, D)

    def encoder_attention(heads):
        if not links.fast:
            return [attend(*head, my_count, VIS, HDIM, True) for head in heads]
        weights = (*enc_mlp[0], *dec_attention[0], *dec_mlp[0])
        nonlocal grad_final
        own_mix, own_weights, other_mix, other_weights, *others = attend_fetch(
            *heads, my_count, VIS, HDIM, weights
        )
        keep, send = halves(lax.optimization_barrier((grad_partial, own_mix))[0], links.place, 0)
        grad_final = keep.astype(F32) + links.over_x(send).astype(F32)
        enc_mlp.append(tuple(others[:2]))
        dec_attention.append(tuple(others[2:4]))
        dec_mlp.append(tuple(others[4:]))
        return (own_mix, own_weights), (other_mix, other_weights)

    stream, enc_saved = block_forward(
        stream, enc_gains, enc_biases, enc_attention, lambda: enc_mlp, encoder_attention, HDIM
    )
    latent = layer_norm(stream, enc_gains[2], enc_biases[2])
    lifted = dot(latent, dec_embed)

    live = jnp.arange(VIS)[None, :] < my_count[:, None]
    select = (my_slots[:, :, None] == jnp.arange(NPATCH)[None, None, :]) & live[:, :, None]
    hidden = 1.0 - jnp.sum(select.astype(F32), axis=1)[:, :, None]
    decoded = (
        jnp.einsum(
            "bsp,bse->bpe",
            select.astype(F32),
            lifted.reshape(own, VIS, DDEC),
            precision=HIGHEST,
        )
        + hidden * mask_token
        + grid_codes(ratios, DDEC)
    ).reshape(own * NPATCH, DDEC)
    decoder_attention = lambda heads: [
        attend(*head, my_count, NPATCH, DHDIM, False) for head in heads
    ]
    decoded, dec_saved = block_forward(
        decoded, dec_gains, dec_biases, dec_attention, lambda: dec_mlp, decoder_attention, DHDIM
    )
    final_own = layer_norm(decoded, dec_gains[2], dec_biases[2])

    final_other = None

    def decoder_attention_back(heads):
        nonlocal final_other
        if not links.fast:
            return [attend_back(*head, NPATCH, DHDIM) for head in heads]
        *grads, final_other = attend_back_swap(*heads, NPATCH, DHDIM, final_own)
        return grads[:3], grads[3:]

    encoder_attention_back = lambda heads: [attend_back(*head, VIS, HDIM) for head in heads]
    grad_in, dec_gain_2, dec_bias_2 = layer_norm_back(grad_final, decoded, dec_gains[2])
    grad_decoded, dec_gain_01, dec_bias_01, dec_grads = block_backward(
        grad_in, dec_gains, dec_attention, dec_mlp, decoder_attention_back, dec_saved
    )

    if links.fast:
        final_all = ordered(links.place, final_own, final_other, 0)
    else:
        final_all = gather_rows(links, final_own)
    reconstructions = row_product(final_all, head_weight).reshape(images, NPATCH, -1)
    head_grad = dot_tn(final_all, cotangent).astype(BF16)
    grad_decoded, head_grad = lax.optimization_barrier((grad_decoded, head_grad))
    head_total = lax.psum(head_grad, "dp").astype(F32)

    grad_grid = grad_decoded.reshape(own, NPATCH, DDEC)
    mask_grad = jnp.sum(hidden * grad_grid, axis=(0, 1))
    grad_lifted = (
        jnp.einsum(
            "bsp,bpe->bse",
            select.astype(BF16),
            grad_grid.astype(BF16),
            preferred_element_type=F32,
        )
        .astype(BF16)
        .reshape(own_slots, DDEC)
    )
    embed_grad = dot_tn(latent, grad_lifted).astype(BF16)
    grad_latent = dot_nt(grad_lifted, dec_embed)

    grad_in, enc_gain_2, enc_bias_2 = layer_norm_back(grad_latent, stream, enc_gains[2])
    grad_stream, enc_gain_01, enc_bias_01, enc_grads = block_backward(
        grad_in, enc_gains, enc_attention, enc_mlp, encoder_attention_back, enc_saved
    )

    grad_embedded = gather_rows(links, grad_stream.astype(BF16))
    patch_grads = [
        dot_tn(picked_multi, grad_embedded).astype(BF16),
        dot_tn(picked_rgb, grad_embedded).astype(BF16),
    ]
    multi_rows = jnp.repeat(band_group == 0, VIS)[:, None]
    back_multi = dot_nt(jnp.where(multi_rows, grad_embedded, zero), patch_weight[0])
    back_rgb = dot_nt(jnp.where(multi_rows, zero, grad_embedded), patch_rgb)
    back_rgb = jnp.where(rgb_valid, back_rgb, 0.0)
    back = back_multi + jnp.pad(back_rgb, ((0, 0), (0, pixel_width - rgb_width)))
    pixel_grad = jnp.einsum(
        "bsp,bsc->bpc",
        one_hot.astype(BF16),
        back.astype(BF16).reshape(images, VIS, pixel_width),
        preferred_element_type=F32,
    )

    dec_qkv_grads, dec_out_grads, dec_up_grads, dec_down_grads = dec_grads
    enc_qkv_grads, enc_out_grads, enc_up_grads, enc_down_grads = enc_grads
    stacked_qkv = lambda grads: [jnp.concatenate(g, 0) for g in grads]
    enc_stack = [
        (stacked_qkv(enc_qkv_grads), 1),
        (enc_out_grads, 0),
        (enc_up_grads, 1),
        (enc_down_grads, 0),
    ]
    dec_stack = [
        (stacked_qkv(dec_qkv_grads), 1),
        (dec_out_grads, 0),
        (dec_up_grads, 1),
        (dec_down_grads, 0),
    ]
    patch_grad = jnp.concatenate(patch_grads, 0)
    small = [*enc_gain_01, enc_gain_2, *enc_bias_01, enc_bias_2]
    small += [*dec_gain_01, dec_gain_2, *dec_bias_01, dec_bias_2, mask_grad]
    small = jnp.concatenate(small)
    if links.fast:
        small_rows = small.shape[0] // DDEC
        shared_rows = -(-(D + small_rows) // 256) * 256
        shared = jnp.concatenate([embed_grad, small.reshape(small_rows, DDEC).astype(BF16)], 0)
        shared = jnp.pad(shared, ((0, shared_rows - D - small_rows), (0, 0)))
        enc_qkv_pair, enc_out_pair, enc_up_pair, enc_down_pair = [g for g, _ in enc_stack]
        crossing = [enc_qkv_pair, enc_up_pair] + [g for g, _ in dec_stack]
        late = [pair[0] for pair in crossing]
        late += [shared, enc_out_pair[0], enc_down_pair[0], patch_grad]
        late = ring_sums(
            late,
            [pair[1] for pair in crossing] + [shared],
            {7: enc_out_pair[1], 8: enc_down_pair[1]},
            {9},
        )
        late, patch_total = [total.astype(F32) for total in late[:9]], late[9]
        enc_totals = [unstack_qkv(late[0]), late[7], late[1], late[8]]
        dec_totals = [unstack_qkv(late[2])] + late[3:6]
        embed_total = late[6][:D]
        small = late[6][D : D + small_rows].reshape(-1)
        patch_total = lax.pad(
            patch_total.astype(F32), 0.0, ((0, pixel_width - rgb_width, 0), (0, 0, 0))
        )
        patch_total = patch_total.reshape(2, pixel_width, D)
    else:
        reduced = []
        for stack in (dec_stack, enc_stack):
            parts = [
                lax.psum_scatter(g[0], "freq", scatter_dimension=axis, tiled=True)
                for g, axis in stack
            ]
            parts = [lax.psum(part, "dp").astype(F32) for part in parts]
            parts[0] = unstack_qkv(parts[0])
            reduced.append(parts)
        dec_totals, enc_totals = reduced
        embed_total = lax.psum(embed_grad, ("dp", "freq")).astype(F32)
        small = lax.psum(small, ("dp", "freq"))
        patch_sum = lax.psum(patch_grad, "dp").astype(F32)
        patch_total = jnp.stack(
            [
                patch_sum[:pixel_width],
                jnp.pad(patch_sum[pixel_width:], ((0, pixel_width - rgb_width), (0, 0))),
            ]
        )
    enc_end, dec_end = 6 * D, 6 * D + 6 * DDEC
    enc_small = small[:enc_end].reshape(2, 3, D)
    dec_small = small[enc_end:dec_end].reshape(2, 3, DDEC)
    return (
        reconstructions,
        pixel_grad,
        patch_total,
        *enc_totals,
        enc_small[0],
        enc_small[1],
        embed_total,
        small[dec_end:],
        *dec_totals,
        dec_small[0],
        dec_small[1],
        head_total,
    )


def solution(mesh):
    return jax.shard_map(
        local,
        mesh=mesh,
        in_specs=(
            P("dp", None, "freq"),
            P("dp"),
            P("dp", None),
            P("dp"),
            P("dp"),
            P(None, "freq", None),
            P(None, None, "freq"),
            P("freq", None),
            P(None, "freq"),
            P("freq", None),
            P(),
            P(),
            P(),
            P(),
            P(None, None, "freq"),
            P("freq", None),
            P(None, "freq"),
            P("freq", None),
            P(),
            P(),
            P(None, "freq"),
            P("dp", None, "freq"),
        ),
        out_specs=(
            P("dp", None, "freq"),
            P("dp", None, "freq"),
            P(None, "freq", None),
            P(None, None, "freq"),
            P("freq", None),
            P(None, "freq"),
            P("freq", None),
            P(),
            P(),
            P(),
            P(),
            P(None, None, "freq"),
            P("freq", None),
            P(None, "freq"),
            P("freq", None),
            P(),
            P(),
            P(None, "freq"),
        ),
        check_vma=False,
    )
```
